32 devices in a mesh: row: 4 (over z), col: 8 (over y, x, core).
Axes of the slice: x: 2, y: 2, z: 4, core: 2. Of those that a mesh axis runs over, the one named last changes fastest.
Arguments:
- matrix: float32 [4, 4, 256, 2, 8, 256], P(None, 'row', None, None, 'col'), may hold values from -6 to 6
- panel_t: float32 [256, 4, 4, 256], P('col', None, 'row'), may hold values from -3 to 3
Outputs:
- updated: float32 [4, 4, 256, 2, 8, 256], P(None, 'row', None, None, 'col')
- vectors: float32 [256, 4, 4, 256], P('col', None, 'row')
- band_block: float32 [256, 256], replicated
- reflector_factor: float32 [256, 256], replicated
The draws below stay inside these ranges and needn't reach their ends.
All inputs are finite; a program needn't handle non-finite values.
Results may differ from the reference program's by a relative error of at most 0.00017.
Values sent between devices are 32-bit elements; how exact they have to be, the bound alone decides.
A program may use at most 64 MiB of HBM per device.

```python
import jax
import jax.numpy as jnp
from jax import lax

NB = 256
TC = 2
TR = 4
N = 4096
N_ROW = 4
N_COL = 8


def draw_panel_t(key, part):
    key = jax.random.fold_in(key, 7)
    base_key, scale_key = jax.random.split(key)
    entries = jnp.clip(jax.random.normal(base_key, (NB, N), jnp.float32), -4.0, 4.0)
    spread = 4.0
    row_scale = jnp.exp(jax.random.uniform(scale_key, (N,), jnp.float32) * jnp.log(spread))
    columns = jnp.arange(N)
    upper_rows = columns < NB
    diagonal = (columns[None, :] == jnp.arange(NB)[:, None]).astype(jnp.float32)
    lower_part = entries * row_scale[None, :] / jnp.sqrt(jnp.float32(N))
    top_part = 2.0 * diagonal + entries / jnp.sqrt(jnp.float32(NB))
    result_panel = jnp.where(upper_rows[None, :], top_part, lower_part)
    return result_panel.reshape(NB, TR, N_ROW, NB)


def block_scale(key, extent, shards, low, high):
    def one(position, shards_of):
        steps = jax.random.uniform(jax.random.fold_in(jax.random.fold_in(key, 6), position), (shards_of,), jnp.float32, low / len(shards), high / len(shards))
        return jnp.repeat(jnp.exp(steps), extent[position] // shards_of).reshape((-1,) + (1,) * (len(extent) - position - 1))

    gain = one(*shards[0])
    for cut in shards[1:]:
        gain = gain * one(*cut)
    return gain


def normal_values(key, shape, scale, most, cuts=(), kind=jnp.bfloat16):
    values = scale * jax.random.normal(key, shape, jnp.float32)
    if cuts:
        values = values * block_scale(key, shape, cuts, -0.22, 0.18)
    return jnp.clip(values, -most, most).astype(kind)


def setup_inputs(seed: int = 0) -> dict:
    splits = jax.random.split(jax.random.key(seed), 3)
    matrix = normal_values(splits[0], (TR, N_ROW, NB, TC, N_COL, NB), 1.0, 6.0, ((1, 4), (4, 8)), jnp.float32)
    panel_t = draw_panel_t(jax.random.fold_in(splits[2], 71), 0)
    return dict(matrix=matrix, panel_t=panel_t)


def matmul(multiplier, multiplicand):
    return jnp.dot(multiplier, multiplicand, precision=lax.Precision.HIGHEST)

def contract_first(multiplier, multiplicand):
    return lax.dot_general(multiplier, multiplicand, (((0,), (0,)), ((), ())), precision=lax.Precision.HIGHEST)

def contract_last(multiplier, multiplicand):
    return lax.dot_general(multiplier, multiplicand, (((1,), (1,)), ((), ())), precision=lax.Precision.HIGHEST)

def lower_solve(factor, right_side, transposed):
    return lax.linalg.triangular_solve(factor, right_side, left_side=True, lower=True, transpose_a=transposed)

def reference(matrix, panel_t):
    dense_matrix = matrix.reshape(N, N)
    panel_cols = panel_t.reshape(NB, N)
    first_factor = jnp.linalg.cholesky(matmul(panel_cols, panel_cols.T))
    orthonormal = lower_solve(first_factor, panel_cols, False)
    band_block = -first_factor.T
    identity = jnp.eye(NB, dtype=jnp.float32)
    vectors_t = jnp.concatenate([orthonormal[:, :NB] + identity, orthonormal[:, NB:]], axis=1)
    top_block = vectors_t[:, :NB]
    top_factor = jnp.linalg.cholesky(contract_first(top_block, top_block))
    reflector = lower_solve(top_factor, lower_solve(top_factor, top_block.T, False), True)
    lower_part = jnp.tril(dense_matrix)
    strict = jnp.tril(dense_matrix, -1)
    products_t = contract_last(vectors_t, lower_part) + matmul(vectors_t, strict)
    curvature = contract_last(vectors_t, products_t)
    mixed_term = matmul(matmul(reflector.T, curvature), reflector)
    update_t = matmul(reflector.T, products_t) - 0.5 * matmul(mixed_term.T, vectors_t)
    correction = contract_first(vectors_t, update_t) + contract_first(update_t, vectors_t)
    updated = jnp.tril(dense_matrix - correction).reshape(matrix.shape)
    return (updated, vectors_t.reshape(panel_t.shape), band_block, reflector)
```

```python
import functools

import jax
import jax.numpy as jnp
from jax import lax
from jax.experimental import pallas as pl
from jax.experimental.pallas import tpu as pltpu
from jax.sharding import PartitionSpec as P

F32 = jnp.float32
VMEM = pltpu.VMEM
HIGHEST = lax.Precision.HIGHEST
HIGH = lax.Precision.HIGH
BLOCK = 64
GROUP = 4


def dot(a, b, over, precision=HIGHEST):
    return lax.dot_general(a, b, (over, ((), ())), precision=precision, preferred_element_type=F32)


NN = ((1,), (0,))
TN = ((0,), (0,))
NT = ((1,), (1,))


def in_vmem(count):
    return [pl.BlockSpec(memory_space=VMEM)] * count


def params(collective=None):
    if collective is None:
        return pltpu.CompilerParams(vmem_limit_bytes=48 << 20)
    return pltpu.CompilerParams(
        vmem_limit_bytes=48 << 20, collective_id=collective, has_side_effects=True
    )


def shape(*dims):
    return jax.ShapeDtypeStruct(dims, F32)


def inverse_factor(block):
    size = block.shape[0]
    row = lax.broadcasted_iota(jnp.int32, (size, 2 * size), 0)
    col = lax.broadcasted_iota(jnp.int32, (size, 2 * size), 1)
    work = jnp.concatenate([block, jnp.zeros_like(block)], axis=1)
    work = jnp.where(col == row + size, 1.0, work)
    scale = jnp.zeros((size, 2 * size), F32)
    for first in range(0, size, GROUP):
        cols = [
            jnp.broadcast_to(work[:, first + t : first + t + 1], (size, 2 * size))
            for t in range(GROUP)
        ]
        for t in range(GROUP):
            j = first + t
            pivot = cols[t][j : j + 1, :]
            factor = jnp.where(row > j, cols[t] * (1.0 / pivot), 0.0)
            for u in range(t + 1, GROUP):
                cols[u] = cols[u] - factor * cols[u][j : j + 1, :]
            work = work - factor * work[j : j + 1, :]
            scale = jnp.where(row == j, lax.rsqrt(pivot), scale)
    return (work * scale)[:, size:]


def factor_into(gram, work, upper_ref, inverse_ref):
    size = gram.shape[0]
    ident = (
        lax.broadcasted_iota(jnp.int32, (size, size), 0)
        == lax.broadcasted_iota(jnp.int32, (size, size), 1)
    ).astype(F32)
    work[:, :size] = gram
    work[:, size:] = ident
    for lo in range(0, size, BLOCK):
        hi = lo + BLOCK
        inv = inverse_factor(work[lo:hi, lo:hi])
        rows = dot(inv, work[lo:hi, :], NN)
        work[lo:hi, :] = rows
        if hi < size:
            work[hi:, :] -= dot(rows[:, hi:size], rows, TN)
    upper = work[:, :size]
    keep = lax.broadcasted_iota(jnp.int32, (size, size), 1) >= lax.broadcasted_iota(
        jnp.int32, (size, size), 0
    )
    upper_ref[...] = jnp.where(keep, upper, 0.0)
    inverse_ref[...] = work[:, size:]


def panel_kernel(gram_ref, top_ref, band_ref, inverse_ref, reflector_ref, work, upper):
    size = gram_ref.shape[0]
    ident = (
        lax.broadcasted_iota(jnp.int32, (size, size), 0)
        == lax.broadcasted_iota(jnp.int32, (size, size), 1)
    ).astype(F32)
    factor_into(gram_ref[...], work, upper, inverse_ref)
    band_ref[...] = -upper[...]
    block = dot(inverse_ref[...], top_ref[...], NN) + ident
    factor_into(dot(block, block, TN), work, upper, reflector_ref)
    inv = reflector_ref[...]
    reflector_ref[...] = dot(inv, dot(inv, block, NT), TN)


def panel_factors(gram, top):
    size = gram.shape[0]
    return pl.pallas_call(
        panel_kernel,
        out_shape=[shape(size, size)] * 3,
        in_specs=in_vmem(2),
        out_specs=in_vmem(3),
        scratch_shapes=[VMEM((size, 2 * size), F32), VMEM((size, size), F32)],
        compiler_params=params(),
    )(gram, top)


def greet(row_peers, col_peers):
    barrier = pltpu.get_barrier_semaphore()
    for peer in row_peers:
        pl.semaphore_signal(
            barrier, inc=1, device_id={"row": peer}, device_id_type=pl.DeviceIdType.MESH
        )
    for peer in col_peers:
        pl.semaphore_signal(
            barrier, inc=1, device_id={"col": peer}, device_id_type=pl.DeviceIdType.MESH
        )
    pl.semaphore_wait(barrier, len(row_peers) + len(col_peers))


def copy_to(axis, peer, src, dst, send, recv):
    return pltpu.make_async_remote_copy(
        src_ref=src,
        dst_ref=dst,
        send_sem=send,
        recv_sem=recv,
        device_id={axis: peer},
        device_id_type=pl.DeviceIdType.MESH,
    )


def others(me, count, step=1):
    return [lax.rem(me + k, count) for k in range(step, count, step)]


def sibling_of(me):
    return me + 1 - 2 * lax.rem(me, 2)


def col_gather(src, out, near_send, near_recv, far_send, far_recv, count):
    me = lax.axis_index("col")
    sibling = sibling_of(me)
    started = []
    for k, peer in enumerate(others(me, count, 2)):
        copy = copy_to("col", peer, src, out.at[me], far_send.at[k], far_recv.at[me])
        copy.start()
        started.append(copy)
    copy = copy_to("col", sibling, src, out.at[me], near_send.at[me], near_recv.at[me])
    copy.start()
    started.append(copy)
    out[me] = src[...]
    for peer in others(me, count, 2):
        copy_to("col", peer, src, out.at[peer], far_send.at[0], far_recv.at[peer]).wait_recv()
        copy = copy_to(
            "col", sibling, out.at[peer], out.at[peer], near_send.at[peer], near_recv.at[peer]
        )
        copy.start()
        started.append(copy)
    for k in range(0, count, 2):
        slot = lax.rem(sibling + k, count)
        copy_to(
            "col", sibling, src, out.at[slot], near_send.at[slot], near_recv.at[slot]
        ).wait_recv()
    return started


def gather_sems(count):
    return [
        pltpu.SemaphoreType.DMA((count,)),
        pltpu.SemaphoreType.DMA((count,)),
        pltpu.SemaphoreType.DMA((count // 2,)),
        pltpu.SemaphoreType.DMA((count,)),
    ]


def gather_kernel(count, src, out, *sems):
    me = lax.axis_index("col")
    greet([], others(me, count, 2) + [sibling_of(me)])
    for copy in col_gather(src, out, *sems, count):
        copy.wait_send()


def gather_panel(block, count):
    return pl.pallas_call(
        functools.partial(gather_kernel, count),
        out_shape=shape(count, *block.shape),
        in_specs=in_vmem(1),
        out_specs=in_vmem(1)[0],
        scratch_shapes=gather_sems(count),
        compiler_params=params(0),
    )(block)


def root_send(value, row_count, root, me, out, send, recv):
    @pl.when(me == root)
    def _():
        for k in range(1, row_count):
            copy_to(
                "row", lax.rem(root + k, row_count), value, out, send.at[k - 1], recv
            ).start()


def root_wait(value, row_count, root, me, out, send, recv):
    @pl.when(me == root)
    def _():
        for k in range(1, row_count):
            copy_to(
                "row", lax.rem(root + k, row_count), value, out, send.at[k - 1], recv
            ).wait_send()
        out[...] = value[...]

    @pl.when(me != root)
    def _():
        copy_to("row", root, value, out, send.at[0], recv).wait_recv()


def row_sum(src, slots, send, recv, row_count):
    me = lax.axis_index("row")
    started = []
    for k, peer in enumerate(others(me, row_count)):
        copy = copy_to("row", peer, src, slots.at[me], send.at[k], recv.at[me])
        copy.start()
        started.append(copy)
    slots[me] = src[...]
    for peer in others(me, row_count):
        copy_to("row", peer, src, slots.at[peer], send.at[0], recv.at[peer]).wait_recv()
    total = slots[0]
    for k in range(1, row_count):
        total = total + slots[k]
    return total, started


def gram_kernel(
    row_count, count, part, pick, out, picked, slots, total, rsend, rrecv, psend, precv, *sems
):
    row, col = lax.axis_index("row"), lax.axis_index("col")
    root = lax.rem(col, row_count)
    greet(others(row, row_count), others(col, count, 2) + [sibling_of(col)])
    value, started = row_sum(part, slots, rsend, rrecv, row_count)
    root_send(pick, row_count, root, row, picked, psend, precv.at[0])
    total[...] = value
    started += col_gather(total, out, *sems, count)
    root_wait(pick, row_count, root, row, picked, psend, precv.at[0])
    for copy in started:
        copy.wait_send()


def gram_sum(part, pick, row_count, count):
    return pl.pallas_call(
        functools.partial(gram_kernel, row_count, count),
        out_shape=[shape(count, *part.shape), shape(*pick.shape)],
        in_specs=in_vmem(2),
        out_specs=in_vmem(2),
        scratch_shapes=[
            VMEM((row_count, *part.shape), F32),
            VMEM(part.shape, F32),
            pltpu.SemaphoreType.DMA((row_count - 1,)),
            pltpu.SemaphoreType.DMA((row_count,)),
            pltpu.SemaphoreType.DMA((row_count - 1,)),
            pltpu.SemaphoreType.DMA((1,)),
            *gather_sems(count),
        ],
        compiler_params=params(1),
    )(part, pick)


def product_kernel(
    row_count, count, groups, tile_cols,
    row_terms, mirror, vectors,
    full, picked, curvature,
    terms, near, mine, far, summed, from_rows, pick, curve, slots, curve_total,
    nsend, nrecv, fsend, frecv, msend, mrecv, rsend, rrecv, psend, precv, *sems,
):
    row, col = lax.axis_index("row"), lax.axis_index("col")
    root = lax.rem(col, row_count)
    slot = col // row_count
    tile = vectors.shape[0]
    span = tile // count
    sibling = sibling_of(col)
    parity = lax.rem(col, 2)
    half = count // 2
    greet(others(row, row_count), others(col, count, 2) + [sibling])

    terms[...] = row_terms[...]

    @pl.when(row != root)
    def _():
        place = lax.rem(row - root + row_count, row_count) - 1
        copy_to("row", root, mirror, from_rows.at[place], msend, mrecv.at[place]).start()

    @pl.when(row == root)
    def _():
        for k in range(row_count - 1):
            copy_to(
                "row", lax.rem(root + k + 1, row_count), mirror, from_rows.at[k], msend, mrecv.at[k]
            ).wait_recv()
        for k in range(tile_cols):
            at = k * groups + slot
            cols = pl.ds(k * tile, tile)
            value = mirror[:, cols]
            for other in range(row_count - 1):
                value = value + from_rows[other, :, cols]
            where = pl.ds(pl.multiple_of(at * tile, tile), tile)
            terms[:, where] += value

    started = []
    for k in range(half):
        j = 2 * k + 1 - parity
        copy = copy_to(
            "col", sibling, terms.at[pl.ds(pl.multiple_of(j * span, span), span)], near.at[k],
            nsend.at[k], nrecv.at[k],
        )
        copy.start()
        started.append(copy)
    for k in range(half):
        copy_to("col", sibling, near.at[k], near.at[k], nsend.at[k], nrecv.at[k]).wait_recv()
        j = 2 * k + parity
        mine[k] = terms[pl.ds(pl.multiple_of(j * span, span), span), :] + near[k]
    place = col // 2
    for k in range(1, half):
        peer = lax.rem(place + k, half)
        copy = copy_to(
            "col", 2 * peer + parity, mine.at[peer], far.at[place], fsend.at[k - 1], frecv.at[place]
        )
        copy.start()
        started.append(copy)
    total = mine[place]
    for k in range(1, half):
        peer = lax.rem(place + k, half)
        copy_to("col", sibling, mine.at[0], far.at[peer], fsend.at[0], frecv.at[peer]).wait_recv()
        total = total + far[peer]
    summed[...] = total

    curve[...] = dot(vectors[...], total, NT)
    started += col_gather(summed, full, *sems[:4], count)
    for k in range(tile_cols):
        at = k * groups + slot
        where = pl.ds(pl.multiple_of(at * tile, tile), tile)
        for j in range(count):
            pick[pl.ds(j * span, span), pl.ds(k * tile, tile)] = full[j, :, where]
    value, more = row_sum(curve, slots, rsend, rrecv, row_count)
    started += more
    root_send(pick, row_count, root, row, picked, psend, precv.at[0])
    curve_total[...] = value
    started += col_gather(curve_total, curvature, *sems[4:], count)
    root_wait(pick, row_count, root, row, picked, psend, precv.at[0])
    for copy in started:
        copy.wait_send()

    @pl.when(row != root)
    def _():
        copy_to("row", root, mirror, from_rows.at[0], msend, mrecv.at[0]).wait_send()


def product_sums(terms, mirror, vectors, row_count, count, groups, tile_cols):
    tile = terms.shape[0]
    span = tile // count
    half = count // 2
    width = terms.shape[1]
    dma = pltpu.SemaphoreType.DMA
    return pl.pallas_call(
        functools.partial(product_kernel, row_count, count, groups, tile_cols),
        out_shape=[shape(count, span, width), shape(*mirror.shape), shape(count, tile, span)],
        in_specs=in_vmem(3),
        out_specs=in_vmem(3),
        scratch_shapes=[
            VMEM(terms.shape, F32),
            VMEM((half, span, width), F32),
            VMEM((half, span, width), F32),
            VMEM((half, span, width), F32),
            VMEM((span, width), F32),
            VMEM((row_count - 1, *mirror.shape), F32),
            VMEM(mirror.shape, F32),
            VMEM((tile, span), F32),
            VMEM((row_count, tile, span), F32),
            VMEM((tile, span), F32),
            dma((half,)),
            dma((half,)),
            dma((half,)),
            dma((half,)),
            dma,
            dma((row_count - 1,)),
            dma((row_count - 1,)),
            dma((row_count,)),
            dma((row_count - 1,)),
            dma((1,)),
            *gather_sems(count),
            *gather_sems(count),
        ],
        compiler_params=params(2),
    )(terms, mirror, vectors)


def pick_slots(block_t, tile_cols, groups, slot_index):
    leading = block_t.shape[0]
    shaped = block_t.reshape(leading, tile_cols, groups, block_t.shape[1] // (tile_cols * groups))
    picked = lax.dynamic_index_in_dim(shaped, slot_index, 2, keepdims=False)
    return picked.reshape(leading, -1)


def body(matrix, panel_t):
    tile_rows = matrix.shape[0]
    tile = matrix.shape[2]
    tile_cols = matrix.shape[3]
    row_count = lax.axis_size("row")
    col_count = lax.axis_size("col")
    row_index = lax.axis_index("row")
    col_index = lax.axis_index("col")
    groups = col_count // row_count
    slot_index = col_index // row_count
    local_rows = tile_rows * tile
    local_cols = tile_cols * tile
    span = tile // col_count
    stored = matrix.reshape(local_rows, local_cols)
    identity = jnp.eye(tile, dtype=F32)
    mine = panel_t.reshape(span, local_rows)

    panel_r = gather_panel(mine, col_count).reshape(tile, local_rows)
    part = dot(mine, panel_r, NT)
    top = jnp.where(row_index == 0, mine[:, :tile], 0.0)
    sums, panel_c = gram_sum(
        jnp.concatenate([part, top], axis=1),
        pick_slots(panel_r, tile_cols, groups, slot_index),
        row_count,
        col_count,
    )
    sums = sums.reshape(tile, 2 * tile)
    band_block, inverse, reflector = panel_factors(sums[:, :tile], sums[:, tile:])

    def with_identity(value, flag):
        head = value[:, :tile] + jnp.where(flag, identity, 0.0)
        return jnp.concatenate([head, value[:, tile:]], axis=1)

    vectors_r = with_identity(dot(inverse, panel_r, NN, HIGH), row_index == 0)
    vectors_c = with_identity(dot(inverse, panel_c, NN, HIGH), col_index == 0)

    row_numbers = jnp.arange(local_rows)
    col_numbers = jnp.arange(local_cols)
    global_row = (row_numbers // tile * row_count + row_index) * tile + row_numbers % tile
    global_col = (col_numbers // tile * col_count + col_index) * tile + col_numbers % tile
    on_lower = global_row[:, None] >= global_col[None, :]
    lower_part = jnp.where(on_lower, stored, 0.0)
    strict_part = jnp.where(global_row[:, None] > global_col[None, :], stored, 0.0)
    terms = dot(vectors_c, lower_part, NT, HIGH)
    mirror = dot(vectors_r, strict_part, NN, HIGH)
    full, products_c, curvature = product_sums(
        terms, mirror, vectors_r, row_count, col_count, groups, tile_cols
    )
    products_r = full.reshape(tile, local_rows)
    curvature = curvature.transpose(1, 0, 2).reshape(tile, tile)
    mixed = dot(dot(reflector, curvature, TN), reflector, NN)
    update_r = dot(reflector, products_r, TN, HIGH) - 0.5 * dot(mixed, vectors_r, TN, HIGH)
    update_c = dot(reflector, products_c, TN, HIGH) - 0.5 * dot(mixed, vectors_c, TN, HIGH)
    correction = dot(
        jnp.concatenate([vectors_r, update_r], axis=0),
        jnp.concatenate([update_c, vectors_c], axis=0),
        TN,
        HIGH,
    )
    updated = jnp.where(on_lower, stored - correction, 0.0).reshape(matrix.shape)
    vectors_out = lax.dynamic_slice_in_dim(vectors_r, col_index * span, span, 0).reshape(
        panel_t.shape
    )
    return (updated, vectors_out, band_block, reflector)


def solution(mesh):
    placed = (P(None, "row", None, None, "col", None), P("col", None, "row", None))
    return jax.shard_map(
        body,
        mesh=mesh,
        in_specs=placed,
        out_specs=(P(None, "row", None, None, "col", None), P("col", None, "row", None), P(), P()),
        check_vma=False,
    )
```

```python
import functools

import jax
import jax.numpy as jnp
from jax import lax
from jax.experimental import pallas as pl
from jax.experimental.pallas import tpu as pltpu
from jax.sharding import PartitionSpec as P

F32 = jnp.float32
VMEM = pltpu.VMEM
HIGHEST = lax.Precision.HIGHEST
BLOCK = 64
GROUP = 4


def dot(a, b, over, precision=HIGHEST):
    return lax.dot_general(a, b, (over, ((), ())), precision=precision, preferred_element_type=F32)


NN = ((1,), (0,))
TN = ((0,), (0,))
NT = ((1,), (1,))


def in_vmem(count):
    return [pl.BlockSpec(memory_space=VMEM)] * count


def params(collective=None):
    if collective is None:
        return pltpu.CompilerParams(vmem_limit_bytes=48 << 20)
    return pltpu.CompilerParams(
        vmem_limit_bytes=48 << 20, collective_id=collective, has_side_effects=True
    )


def shape(*dims):
    return jax.ShapeDtypeStruct(dims, F32)


def inverse_factor(block):
    size = block.shape[0]
    row = lax.broadcasted_iota(jnp.int32, (size, 2 * size), 0)
    col = lax.broadcasted_iota(jnp.int32, (size, 2 * size), 1)
    work = jnp.concatenate([block, jnp.zeros_like(block)], axis=1)
    work = jnp.where(col == row + size, 1.0, work)
    scale = jnp.zeros((size, 2 * size), F32)
    for first in range(0, size, GROUP):
        cols = [
            jnp.broadcast_to(work[:, first + t : first + t + 1], (size, 2 * size))
            for t in range(GROUP)
        ]
        for t in range(GROUP):
            j = first + t
            pivot = cols[t][j : j + 1, :]
            factor = jnp.where(row > j, cols[t] * (1.0 / pivot), 0.0)
            for u in range(t + 1, GROUP):
                cols[u] = cols[u] - factor * cols[u][j : j + 1, :]
            work = work - factor * work[j : j + 1, :]
            scale = jnp.where(row == j, lax.rsqrt(pivot), scale)
    return (work * scale)[:, size:]


def dot3(a, b, over):
    ah, bh = a.astype(jnp.bfloat16), b.astype(jnp.bfloat16)
    al, bl = (a - ah.astype(F32)).astype(jnp.bfloat16), (b - bh.astype(F32)).astype(jnp.bfloat16)
    one = functools.partial(dot, over=over, precision=None)
    return one(ah, bl) + one(al, bh) + one(ah, bh)


def unit(size):
    row = lax.broadcasted_iota(jnp.int32, (size, size), 0)
    return (row == lax.broadcasted_iota(jnp.int32, (size, size), 1)).astype(F32)


def factor_steps(gram, work):
    size = gram.shape[0]
    work[:, :size] = gram
    work[:, size:] = unit(size)
    for lo in range(0, size, BLOCK):
        hi = lo + BLOCK
        inv = inverse_factor(work[lo:hi, lo:hi])
        rows = dot(inv, work[lo:hi, :], NN)
        work[lo:hi, :] = rows
        if hi < size:
            work[hi:, :] -= dot(rows[:, hi:size], rows, TN)
        yield


def greet(row_peers, col_peers):
    barrier = pltpu.get_barrier_semaphore()
    for peer in row_peers:
        pl.semaphore_signal(
            barrier, inc=1, device_id={"row": peer}, device_id_type=pl.DeviceIdType.MESH
        )
    for peer in col_peers:
        pl.semaphore_signal(
            barrier, inc=1, device_id={"col": peer}, device_id_type=pl.DeviceIdType.MESH
        )
    pl.semaphore_wait(barrier, len(row_peers) + len(col_peers))


def copy_to(axis, peer, src, dst, send, recv):
    return pltpu.make_async_remote_copy(
        src_ref=src,
        dst_ref=dst,
        send_sem=send,
        recv_sem=recv,
        device_id={axis: peer},
        device_id_type=pl.DeviceIdType.MESH,
    )


def others(me, count, step=1):
    return [lax.rem(me + k, count) for k in range(step, count, step)]


def sibling_of(me):
    return me + 1 - 2 * lax.rem(me, 2)


class Gather:
    def __init__(self, src, out, sems, count):
        self.src, self.out, self.count = src, out, count
        self.near_send, self.near_recv, self.far_send, self.far_recv = sems
        self.me = lax.axis_index("col")
        self.sibling = sibling_of(self.me)
        self.started = []

    def near(self, src, slot):
        return copy_to(
            "col", self.sibling, src, self.out.at[slot], self.near_send.at[slot],
            self.near_recv.at[slot],
        )

    def far(self, peer, slot, k):
        return copy_to(
            "col", peer, self.src, self.out.at[slot], self.far_send.at[k], self.far_recv.at[slot]
        )

    def start(self):
        for k, peer in enumerate(others(self.me, self.count, 2)):
            self.started.append(self.far(peer, self.me, k))
            self.started[-1].start()
        self.started.append(self.near(self.src, self.me))
        self.started[-1].start()
        self.out[self.me] = self.src[...]

    def finish(self):
        for peer in others(self.me, self.count, 2):
            self.far(peer, peer, 0).wait_recv()
            self.started.append(self.near(self.out.at[peer], peer))
            self.started[-1].start()
        for k in range(0, self.count, 2):
            self.near(self.src, lax.rem(self.sibling + k, self.count)).wait_recv()

    def drain(self):
        for copy in self.started:
            copy.wait_send()


class RowSum:
    def __init__(self, src, slots, send, recv, count):
        self.src, self.slots, self.send, self.recv, self.count = src, slots, send, recv, count
        self.me = lax.axis_index("row")

    def copy(self, peer, slot, k):
        return copy_to(
            "row", peer, self.src, self.slots.at[slot], self.send.at[k], self.recv.at[slot]
        )

    def start(self):
        for k, peer in enumerate(others(self.me, self.count)):
            self.copy(peer, self.me, k).start()
        self.slots[self.me] = self.src[...]

    def finish(self):
        for peer in others(self.me, self.count):
            self.copy(peer, peer, 0).wait_recv()

    def total(self):
        total = self.slots[0]
        for k in range(1, self.count):
            total = total + self.slots[k]
        return total

    def drain(self):
        for k, peer in enumerate(others(self.me, self.count)):
            self.copy(peer, self.me, k).wait_send()


DMA = pltpu.SemaphoreType.DMA


def gather_sems(count):
    return [DMA((count,)), DMA((count,)), DMA((count // 2,)), DMA((count,))]


def row_sems(count):
    return [DMA((count - 1,)), DMA((count,))]


def panel_kernel(
    row_count, count, groups, tile_cols,
    mine, panel_r, panel_c, top, band, inverse,
    panel_z, part, slots, part_total, gram, work, csend, crecv, *sems,
):
    row, col = lax.axis_index("row"), lax.axis_index("col")
    span = mine.shape[0]
    tile = span * count
    peers = others(col, count)
    greet(others(row, row_count), peers)
    gather_r = Gather(mine, panel_r, sems[0:4], count)
    gather_g = Gather(part_total, gram, sems[4:8], count)
    rows_z = RowSum(mine, panel_z, *sems[8:10], row_count)
    rows_g = RowSum(part, slots, *sems[10:12], row_count)
    gather_r.start()
    rows_z.start()
    gather_r.finish()
    part[...] = dot(mine[...], panel_r[...].reshape(tile, -1), NT)
    rows_g.start()
    rows_g.finish()
    part_total[...] = rows_g.total()
    gather_g.start()
    rows_z.finish()
    gather_g.finish()

    def tiles_for(target):
        root, slot = lax.rem(target, row_count), target // row_count
        for k in range(tile_cols):
            start = pl.multiple_of((k * groups + slot) * tile, tile)
            yield panel_z.at[root, :, pl.ds(start, tile)], pl.ds(k * tile, tile)

    started = []
    for n, peer in enumerate(peers):
        for k, (src, at) in enumerate(tiles_for(peer)):
            started.append(
                copy_to("col", peer, src, panel_c.at[col, :, at], csend.at[n, k], crecv.at[col, k])
            )
        started.append(
            copy_to(
                "col", peer, panel_z.at[0, :, pl.ds(0, tile)], top.at[col],
                csend.at[n, tile_cols], crecv.at[col, tile_cols],
            )
        )
    for copy in started:
        copy.start()
    for src, at in tiles_for(col):
        panel_c[col, :, at] = src[...]
    top[col] = panel_z[0, :, :tile]

    for _ in factor_steps(gram[...].reshape(tile, tile), work):
        pass
    keep = lax.broadcasted_iota(jnp.int32, (tile, tile), 1) >= lax.broadcasted_iota(
        jnp.int32, (tile, tile), 0
    )
    band[...] = jnp.where(keep, -work[:, :tile], 0.0)
    inverse[...] = work[:, tile:]
    for peer in peers:
        for k, (src, at) in enumerate(tiles_for(col)):
            copy_to(
                "col", peer, src, panel_c.at[peer, :, at], csend.at[0, k], crecv.at[peer, k]
            ).wait_recv()
        copy_to(
            "col", peer, top.at[col], top.at[peer], csend.at[0, 0], crecv.at[peer, tile_cols]
        ).wait_recv()
    for each in (gather_r, gather_g, rows_z, rows_g, *started):
        each.drain() if hasattr(each, "drain") else each.wait_send()


def panel_step(mine, row_count, count, groups, tile_cols):
    span, width = mine.shape
    tile = span * count
    return pl.pallas_call(
        functools.partial(panel_kernel, row_count, count, groups, tile_cols),
        out_shape=[
            shape(count, span, width),
            shape(count, span, tile_cols * tile),
            shape(count, span, tile),
            shape(tile, tile),
            shape(tile, tile),
        ],
        in_specs=in_vmem(1),
        out_specs=in_vmem(5),
        scratch_shapes=[
            VMEM((row_count, span, width), F32),
            VMEM((span, tile), F32),
            VMEM((row_count, span, tile), F32),
            VMEM((span, tile), F32),
            VMEM((count, span, tile), F32),
            VMEM((tile, 2 * tile), F32),
            DMA((count - 1, tile_cols + 1)),
            DMA((count, tile_cols + 1)),
            *gather_sems(count),
            *gather_sems(count),
            *row_sems(row_count),
            *row_sems(row_count),
        ],
        compiler_params=params(0),
    )(mine)


PARTS = 4


def product_kernel(
    row_count, count, groups, tile_cols,
    lines, panel_r, panel_c, top, inverse,
    out_r, out_c, update_r, update_c, reflector, out_mine,
    mirror, low, high, acc, near, mine, far, summed, full, picked, curve, slots, curve_total,
    curvature, work,
    chain_send, low_recv, high_recv, nsend, nrecv, fsend, frecv, up_send, down_send, precv, *sems,
):
    row, col = lax.axis_index("row"), lax.axis_index("col")
    root, slot = lax.rem(col, row_count), col // row_count
    tile, width = panel_r.shape
    halves, _, sub, _ = acc.shape
    span = tile // count
    per = tile // PARTS // sub
    sibling, parity, half = sibling_of(col), lax.rem(col, 2), count // 2
    greet(others(row, row_count), others(col, count, 2) + [sibling])

    inv = inverse[...]
    out_r[...] = dot3(inv, panel_r[...], NN)
    out_c[...] = dot3(inv, panel_c[...], NN)

    @pl.when(row == 0)
    def _():
        out_r[:, :tile] += unit(tile)

    @pl.when(col == 0)
    def _():
        out_c[:, :tile] += unit(tile)

    vectors = out_r[...]
    matrix, global_row, global_col = read_matrix(lines, width, tile, row_count, count, tile_cols)
    products = dot3(vectors, jnp.where(global_row > global_col, matrix, 0.0), NN)
    mirror[...] = products.reshape(mirror.shape)

    from_low = (row > 0) & (row <= root)
    from_high = (row < row_count - 1) & (row >= root)
    is_end = (row != root) & ((row == 0) | (row == row_count - 1))

    def hop_up(q):
        peer = jnp.minimum(row + 1, row_count - 1)
        return copy_to("row", peer, mirror.at[q], low.at[q], chain_send.at[q], low_recv.at[q])

    def hop_down(q):
        peer = jnp.maximum(row - 1, 0)
        return copy_to("row", peer, mirror.at[q], high.at[q], chain_send.at[q], high_recv.at[q])

    def hop(q, go, act):
        pl.when(go & (row < root))(lambda: act(hop_up(q)))
        pl.when(go & (row > root))(lambda: act(hop_down(q)))

    for q in range(PARTS):
        hop(q, is_end, lambda copy: copy.start())

    terms = dot3(out_c[...], jnp.where(global_row >= global_col, matrix, 0.0), NT)
    acc[...] = terms.reshape(acc.shape)
    started = []

    def chunk_of(q):
        return q * halves // PARTS, (q * per) % count

    for q in range(PARTS):

        @pl.when(from_low)
        def _():
            copy_to(
                "row", jnp.maximum(row - 1, 0), mirror.at[q], low.at[q], chain_send.at[q],
                low_recv.at[q],
            ).wait_recv()
            mirror[q] += low[q]

        @pl.when(from_high)
        def _():
            copy_to(
                "row", jnp.minimum(row + 1, row_count - 1), mirror.at[q], high.at[q],
                chain_send.at[q], high_recv.at[q],
            ).wait_recv()
            mirror[q] += high[q]

        hop(q, jnp.logical_not(is_end), lambda copy: copy.start())
        h, first = chunk_of(q)

        @pl.when(row == root)
        def _():
            for k in range(tile_cols):
                where = pl.ds(pl.multiple_of((k * groups + slot) * tile, tile), tile)
                value = mirror[q, :, k * tile : (k + 1) * tile].reshape(per, sub, tile)
                acc[h, first : first + per, :, where] += value

        if (q + 1) % (PARTS // halves) == 0:
            for k in range(half):
                j = 2 * k + 1 - parity
                started.append(
                    copy_to("col", sibling, acc.at[h, j], near.at[h, k], nsend.at[h, k], nrecv.at[h, k])
                )
                started[-1].start()

    block = dot(inv, top[...], NN) + unit(tile)
    factor = factor_steps(dot(block, block, TN), work)

    place = col // 2
    for h in range(halves):
        for k in range(half):
            copy_to(
                "col", sibling, acc.at[h, 0], near.at[h, k], nsend.at[h, k], nrecv.at[h, k]
            ).wait_recv()
            mine[h, k] = acc[h, 2 * k + parity] + near[h, k]
        for k, peer in enumerate(others(place, half)):
            started.append(
                copy_to(
                    "col", 2 * peer + parity, mine.at[h, peer], far.at[h, place], fsend.at[h, k],
                    frecv.at[h, place],
                )
            )
            started[-1].start()
    next(factor, None)

    gathers = [
        Gather(summed.at[h], full.at[h], sems[4 * h : 4 * h + 4], count) for h in range(halves)
    ]
    for h in range(halves):
        total = mine[h, place]
        for peer in others(place, half):
            copy_to(
                "col", 2 * peer + parity, mine.at[h, 0], far.at[h, peer], fsend.at[h, 0],
                frecv.at[h, peer],
            ).wait_recv()
            total = total + far[h, peer]
        summed[h] = total
        gathers[h].start()

    sems = sems[4 * halves :]
    curve[...] = dot3(summed[...].reshape(span, width), vectors, NT)
    curve_sum = RowSum(curve, slots, *sems[:2], row_count)
    curve_gather = Gather(curve_total, curvature, sems[2:6], count)
    curve_sum.start()
    next(factor, None)

    def pass_up(q):
        peer = jnp.minimum(row + 1, row_count - 1)
        return copy_to("row", peer, picked.at[q], picked.at[q], up_send.at[q], precv.at[q])

    def pass_down(q):
        peer = jnp.maximum(row - 1, 0)
        return copy_to("row", peer, picked.at[q], picked.at[q], down_send.at[q], precv.at[q])

    def pass_on(q, go, act):
        pl.when(go & (row >= root) & (row < row_count - 1))(lambda: act(pass_up(q)))
        pl.when(go & (row <= root) & (row > 0))(lambda: act(pass_down(q)))

    def pick(q):
        h, first = chunk_of(q)

        @pl.when(row == root)
        def _():
            for k in range(tile_cols):
                where = pl.ds(pl.multiple_of((k * groups + slot) * tile, tile), tile)
                value = full[h, first : first + per, :, where]
                picked[q, :, k * tile : (k + 1) * tile] = value.reshape(tile // PARTS, tile)

        pass_on(q, row == root, lambda copy: copy.start())

    for h in range(halves):
        gathers[h].finish()
        for q in range(h * PARTS // halves, (h + 1) * PARTS // halves):
            pick(q)
        if h == 0:
            curve_sum.finish()
            curve_total[...] = curve_sum.total()
            curve_gather.start()
    curve_gather.finish()
    for q in range(PARTS):
        pl.when(row > root)(lambda: pass_down(q).wait_recv())
        pl.when(row < root)(lambda: pass_up(q).wait_recv())
        pass_on(q, row != root, lambda copy: copy.start())
        if q in (0, PARTS - 1):
            next(factor, None)
    for _ in factor:
        pass

    inv2 = work[:, tile:]
    reflect = dot(inv2, dot(inv2, block, NT), TN)
    reflector[...] = reflect
    pieces = curvature[...]
    curvature_t = jnp.concatenate(
        [pieces[:, h * sub : (h + 1) * sub].reshape(tile // halves, tile) for h in range(halves)],
        axis=0,
    )
    mixed = -0.5 * dot(dot(reflect, curvature_t, TN), reflect, NN)
    update_r[...] = dot3(reflect, full[...].reshape(tile, width), TN) + dot3(mixed, vectors, NN)
    update_c[...] = dot3(reflect, picked[...].reshape(tile, -1), TN) + dot3(mixed, out_c[...], NN)
    out_mine[...] = out_r[pl.ds(pl.multiple_of(col * span, span), span), :]

    for q in range(PARTS):
        hop(q, row != root, lambda copy: copy.wait_send())
        pass_on(q, row >= 0, lambda copy: copy.wait_send())
    curve_sum.drain()
    for each in (*gathers, curve_gather):
        each.drain()
    for copy in started:
        copy.wait_send()


def read_matrix(lines, rows, tile, row_count, count, tile_cols):
    row, col = lax.axis_index("row"), lax.axis_index("col")
    strips = tile_cols * tile // 128
    matrix = jnp.concatenate(
        [lines[pl.ds(k, rows, stride=strips), :] for k in range(strips)], axis=1
    )
    r = lax.broadcasted_iota(jnp.int32, matrix.shape, 0)
    c = lax.broadcasted_iota(jnp.int32, matrix.shape, 1)
    global_row = (r // tile * row_count + row) * tile + r % tile
    global_col = (c // tile * count + col) * tile + c % tile
    return matrix, global_row, global_col


def product_step(lines, panel_r, panel_c, top, inverse, row_count, count, groups, tile_cols):
    tile, width = panel_r.shape
    cols = panel_c.shape[1]
    span, half = tile // count, count // 2
    halves = 2 if span % 16 == 0 else 1
    sub = span // halves
    part = (PARTS, tile // PARTS, cols)
    return pl.pallas_call(
        functools.partial(product_kernel, row_count, count, groups, tile_cols),
        out_shape=[
            shape(tile, width),
            shape(tile, cols),
            shape(tile, width),
            shape(tile, cols),
            shape(tile, tile),
            shape(span, width),
        ],
        in_specs=in_vmem(5),
        out_specs=in_vmem(6),
        scratch_shapes=[
            VMEM(part, F32),
            VMEM(part, F32),
            VMEM(part, F32),
            VMEM((halves, count, sub, width), F32),
            VMEM((halves, half, sub, width), F32),
            VMEM((halves, half, sub, width), F32),
            VMEM((halves, half, sub, width), F32),
            VMEM((halves, sub, width), F32),
            VMEM((halves, count, sub, width), F32),
            VMEM(part, F32),
            VMEM((span, tile), F32),
            VMEM((row_count, span, tile), F32),
            VMEM((span, tile), F32),
            VMEM((count, span, tile), F32),
            VMEM((tile, 2 * tile), F32),
            DMA((PARTS,)),
            DMA((PARTS,)),
            DMA((PARTS,)),
            DMA((halves, half)),
            DMA((halves, half)),
            DMA((halves, half)),
            DMA((halves, half)),
            DMA((PARTS,)),
            DMA((PARTS,)),
            DMA((PARTS,)),
            *(gather_sems(count) * halves),
            *row_sems(row_count),
            *gather_sems(count),
        ],
        compiler_params=params(1),
    )(lines, panel_r, panel_c, top, inverse)


def update_kernel(row_count, count, tile_cols, where, lines, yr, xr, yc, xc, out):
    tile = yr.shape[0]
    strips = tile_cols * tile // 128
    step = pl.program_id(0)
    left = jnp.concatenate([yr[...], xr[...]], axis=0)
    right = jnp.concatenate([xc[...], yc[...]], axis=0)
    correction = dot3(left, right, TN)
    r = lax.broadcasted_iota(jnp.int32, (tile, 128), 0)
    c = lax.broadcasted_iota(jnp.int32, (tile, 128), 1)
    global_row = (step * row_count + where[0]) * tile + r
    for k in range(strips):
        first = (k * 128 // tile * count + where[1]) * tile + k * 128 % tile
        rows = pl.ds(k, tile, stride=strips)
        value = lines[rows, :] - correction[:, k * 128 : (k + 1) * 128]
        out[rows, :] = jnp.where(global_row >= first + c, value, 0.0)


def update_step(where, lines, yr, xr, yc, xc, row_count, count, tile_cols):
    tile, width = yr.shape
    steps = width // tile
    block = (lines.shape[0] // steps, 128)
    strip = pl.BlockSpec((tile, tile), lambda i: (0, i))
    whole = pl.BlockSpec(yc.shape, lambda i: (0, 0))
    lined = pl.BlockSpec(block, lambda i: (i, 0))
    return pl.pallas_call(
        functools.partial(update_kernel, row_count, count, tile_cols),
        grid=(steps,),
        out_shape=shape(*lines.shape),
        in_specs=[pl.BlockSpec(memory_space=pltpu.SMEM), lined, strip, strip, whole, whole],
        out_specs=lined,
        compiler_params=params(),
    )(where, lines, yr, xr, yc, xc)


def body(matrix, panel_t):
    tile_rows, _, tile, tile_cols = matrix.shape[:4]
    row_count, count = lax.axis_size("row"), lax.axis_size("col")
    groups = count // row_count
    span, width = tile // count, tile_rows * tile
    lines = matrix.reshape(-1, 128)
    sizes = (row_count, count, groups, tile_cols)
    panel_r, panel_c, top, band_block, inverse = panel_step(panel_t.reshape(span, width), *sizes)
    yr, yc, xr, xc, reflector, vectors = product_step(
        lines,
        panel_r.reshape(tile, width),
        panel_c.reshape(tile, -1),
        top.reshape(tile, tile),
        inverse,
        *sizes,
    )
    where = jnp.stack([lax.axis_index("row"), lax.axis_index("col")])
    updated = update_step(where, lines, yr, xr, yc, xc, row_count, count, tile_cols)
    return (updated.reshape(matrix.shape), vectors.reshape(panel_t.shape), band_block, reflector)


def solution(mesh):
    placed = (P(None, "row", None, None, "col", None), P("col", None, "row", None))
    return jax.shard_map(
        body,
        mesh=mesh,
        in_specs=placed,
        out_specs=(P(None, "row", None, None, "col", None), P("col", None, "row", None), P(), P()),
        check_vma=False,
    )
```

```python
import functools

import jax
import jax.numpy as jnp
from jax import lax
from jax.experimental import pallas as pl
from jax.experimental.pallas import tpu as pltpu
from jax.sharding import PartitionSpec as P

F32 = jnp.float32
VMEM = pltpu.VMEM
HIGHEST = lax.Precision.HIGHEST
BLOCK = 64
GROUP = 4


def dot(a, b, over, precision=HIGHEST):
    return lax.dot_general(a, b, (over, ((), ())), precision=precision, preferred_element_type=F32)


NN = ((1,), (0,))
TN = ((0,), (0,))
NT = ((1,), (1,))


def in_vmem(count):
    return [pl.BlockSpec(memory_space=VMEM)] * count


def params(collective=None):
    if collective is None:
        return pltpu.CompilerParams(vmem_limit_bytes=48 << 20)
    return pltpu.CompilerParams(
        vmem_limit_bytes=48 << 20, collective_id=collective, has_side_effects=True
    )


def shape(*dims):
    return jax.ShapeDtypeStruct(dims, F32)


def inverse_factor(block):
    size = block.shape[0]
    row = lax.broadcasted_iota(jnp.int32, (size, 2 * size), 0)
    col = lax.broadcasted_iota(jnp.int32, (size, 2 * size), 1)
    work = jnp.concatenate([block, jnp.zeros_like(block)], axis=1)
    work = jnp.where(col == row + size, 1.0, work)
    scale = jnp.zeros((size, 2 * size), F32)
    for first in range(0, size, GROUP):
        cols = [
            jnp.broadcast_to(work[:, first + t : first + t + 1], (size, 2 * size))
            for t in range(GROUP)
        ]
        for t in range(GROUP):
            j = first + t
            pivot = cols[t][j : j + 1, :]
            guess = pl.reciprocal(pivot, approx=True)
            factor = jnp.where(row > j, cols[t] * (guess * (2.0 - pivot * guess)), 0.0)
            for u in range(t + 1, GROUP):
                cols[u] = cols[u] - factor * cols[u][j : j + 1, :]
            work = work - factor * work[j : j + 1, :]
            scale = jnp.where(row == j, lax.rsqrt(pivot), scale)
    return (work * scale)[:, size:]


def dot3(a, b, over):
    ah, bh = a.astype(jnp.bfloat16), b.astype(jnp.bfloat16)
    al, bl = (a - ah.astype(F32)).astype(jnp.bfloat16), (b - bh.astype(F32)).astype(jnp.bfloat16)
    one = functools.partial(dot, over=over, precision=None)
    return one(ah, bl) + one(al, bh) + one(ah, bh)


def unit(size):
    row = lax.broadcasted_iota(jnp.int32, (size, size), 0)
    return (row == lax.broadcasted_iota(jnp.int32, (size, size), 1)).astype(F32)


def factor_steps(gram, work):
    size = gram.shape[0]
    work[:, :size] = gram
    work[:, size:] = unit(size)
    for lo in range(0, size, BLOCK):
        hi = lo + BLOCK
        inv = inverse_factor(work[lo:hi, lo:hi])
        rows = dot(inv, work[lo:hi, :], NN)
        work[lo:hi, :] = rows
        if hi < size:
            work[hi:, :] -= dot(rows[:, hi:size], rows, TN)
        yield


def greet(row_peers, col_peers):
    barrier = pltpu.get_barrier_semaphore()
    for peer in row_peers:
        pl.semaphore_signal(
            barrier, inc=1, device_id={"row": peer}, device_id_type=pl.DeviceIdType.MESH
        )
    for peer in col_peers:
        pl.semaphore_signal(
            barrier, inc=1, device_id={"col": peer}, device_id_type=pl.DeviceIdType.MESH
        )
    pl.semaphore_wait(barrier, len(row_peers) + len(col_peers))


def copy_to(axis, peer, src, dst, send, recv):
    return pltpu.make_async_remote_copy(
        src_ref=src,
        dst_ref=dst,
        send_sem=send,
        recv_sem=recv,
        device_id={axis: peer},
        device_id_type=pl.DeviceIdType.MESH,
    )


def others(me, count, step=1):
    return [lax.rem(me + k, count) for k in range(step, count, step)]


def sibling_of(me):
    return me + 1 - 2 * lax.rem(me, 2)


class Gather:
    def __init__(self, src, out, sems, count):
        self.src, self.out, self.count = src, out, count
        self.near_send, self.near_recv, self.far_send, self.far_recv = sems
        self.me = lax.axis_index("col")
        self.sibling = sibling_of(self.me)
        self.started = []

    def near(self, src, slot):
        return copy_to(
            "col", self.sibling, src, self.out.at[slot], self.near_send.at[slot],
            self.near_recv.at[slot],
        )

    def far(self, peer, slot, k):
        return copy_to(
            "col", peer, self.src, self.out.at[slot], self.far_send.at[k], self.far_recv.at[slot]
        )

    def start(self):
        for k, peer in enumerate(others(self.me, self.count, 2)):
            self.started.append(self.far(peer, self.me, k))
            self.started[-1].start()
        self.started.append(self.near(self.src, self.me))
        self.started[-1].start()
        self.out[self.me] = self.src[...]

    def finish(self):
        for peer in others(self.me, self.count, 2):
            self.far(peer, peer, 0).wait_recv()
            self.started.append(self.near(self.out.at[peer], peer))
            self.started[-1].start()
        for k in range(0, self.count, 2):
            self.near(self.src, lax.rem(self.sibling + k, self.count)).wait_recv()

    def drain(self):
        for copy in self.started:
            copy.wait_send()


class RowSum:
    def __init__(self, src, slots, send, recv, count):
        self.src, self.slots, self.send, self.recv, self.count = src, slots, send, recv, count
        self.me = lax.axis_index("row")

    def copy(self, peer, slot, k):
        return copy_to(
            "row", peer, self.src, self.slots.at[slot], self.send.at[k], self.recv.at[slot]
        )

    def start(self):
        for k, peer in enumerate(others(self.me, self.count)):
            self.copy(peer, self.me, k).start()
        self.slots[self.me] = self.src[...]

    def finish(self):
        for peer in others(self.me, self.count):
            self.copy(peer, peer, 0).wait_recv()

    def total(self):
        total = self.slots[0]
        for k in range(1, self.count):
            total = total + self.slots[k]
        return total

    def drain(self):
        for k, peer in enumerate(others(self.me, self.count)):
            self.copy(peer, self.me, k).wait_send()


DMA = pltpu.SemaphoreType.DMA


def gather_sems(count):
    return [DMA((count,)), DMA((count,)), DMA((count // 2,)), DMA((count,))]


def row_sems(count):
    return [DMA((count - 1,)), DMA((count,))]


def panel_kernel(
    row_count, count, groups, tile_cols,
    own_lines, lines_hbm, panel_r, panel_c, top, band, inverse, mirror_sum,
    mine, lines, mirror, from_rows, panel_z, part, slots, part_total, gram, work,
    load, msend, mrecv, csend, crecv, *sems,
):
    row, col = lax.axis_index("row"), lax.axis_index("col")
    span, width = mine.shape
    tile = span * count
    peers = others(col, count)
    root = lax.rem(col, row_count)
    fetch = pltpu.make_async_copy(lines_hbm, lines, load)
    fetch.start()
    strips = width // 128
    for k in range(strips):
        mine[:, k * 128 : (k + 1) * 128] = own_lines[pl.ds(k, span, stride=strips), :]
    greet(others(row, row_count), peers)
    gather_r = Gather(mine, panel_r, sems[0:4], count)
    gather_g = Gather(part_total, gram, sems[4:8], count)
    rows_z = RowSum(mine, panel_z, *sems[8:10], row_count)
    rows_g = RowSum(part, slots, *sems[10:12], row_count)
    gather_r.start()
    rows_z.start()
    gather_r.finish()
    part[...] = dot(mine[...], panel_r[...].reshape(tile, -1), NT)
    rows_g.start()
    fetch.wait()
    matrix, global_row, global_col = read_matrix(lines, width, tile, row_count, count, tile_cols)
    strict = jnp.where(global_row > global_col, matrix, 0.0)
    mirror[...] = dot3(panel_r[...].reshape(tile, width), strict, NN)
    rows_g.finish()
    part_total[...] = rows_g.total()
    gather_g.start()
    rows_z.finish()
    gather_g.finish()

    place = jnp.maximum(lax.rem(row - root + row_count, row_count) - 1, 0)

    def to_root():
        return copy_to("row", root, mirror, from_rows.at[place], msend, mrecv.at[place])

    pl.when(row != root)(lambda: to_root().start())

    def tiles_for(target):
        root, slot = lax.rem(target, row_count), target // row_count
        for k in range(tile_cols):
            start = pl.multiple_of((k * groups + slot) * tile, tile)
            yield panel_z.at[root, :, pl.ds(start, tile)], pl.ds(k * tile, tile)

    started = []
    for n, peer in enumerate(peers):
        for k, (src, at) in enumerate(tiles_for(peer)):
            started.append(
                copy_to("col", peer, src, panel_c.at[col, :, at], csend.at[n, k], crecv.at[col, k])
            )
        started.append(
            copy_to(
                "col", peer, panel_z.at[0, :, pl.ds(0, tile)], top.at[col],
                csend.at[n, tile_cols], crecv.at[col, tile_cols],
            )
        )
    for copy in started:
        copy.start()
    for src, at in tiles_for(col):
        panel_c[col, :, at] = src[...]
    top[col] = panel_z[0, :, :tile]

    for _ in factor_steps(gram[...].reshape(tile, tile), work):
        pass
    keep = lax.broadcasted_iota(jnp.int32, (tile, tile), 1) >= lax.broadcasted_iota(
        jnp.int32, (tile, tile), 0
    )
    upper = jnp.where(keep, work[:, :tile], 0.0)
    band[...] = -upper
    inverse[...] = work[:, tile:]
    factor = upper.T
    for peer in peers:
        for k, (src, at) in enumerate(tiles_for(col)):
            copy_to(
                "col", peer, src, panel_c.at[peer, :, at], csend.at[0, k], crecv.at[peer, k]
            ).wait_recv()
        copy_to(
            "col", peer, top.at[col], top.at[peer], csend.at[0, 0], crecv.at[peer, tile_cols]
        ).wait_recv()
    for each in (gather_r, gather_g, rows_z, rows_g, *started):
        each.drain() if hasattr(each, "drain") else each.wait_send()

    @pl.when(row == 0)
    def _():
        panel_r[:, :, :tile] += factor.reshape(count, span, tile)

    @pl.when(col == 0)
    def _():
        panel_c[:, :, :tile] += factor.reshape(count, span, tile)

    @pl.when(row != root)
    def _():
        to_root().wait_send()
        mirror_sum[...] = mirror[...]

    @pl.when(row == root)
    def _():
        total = mirror[...]
        for k in range(row_count - 1):
            copy_to(
                "row", lax.rem(root + k + 1, row_count), mirror, from_rows.at[k], msend, mrecv.at[k]
            ).wait_recv()
            total = total + from_rows[k]
        mirror_sum[...] = total

    @pl.when((row == 0) & (col == 0))
    def _():
        mirror_sum[:, :tile] += dot3(factor, strict[:tile, :tile], NN)


def panel_step(own_lines, lines, tile, row_count, count, groups, tile_cols):
    span = tile // count
    width = own_lines.shape[0] * 128 // span
    cols = tile_cols * tile
    return pl.pallas_call(
        functools.partial(panel_kernel, row_count, count, groups, tile_cols),
        out_shape=[
            shape(count, span, width),
            shape(count, span, tile_cols * tile),
            shape(count, span, tile),
            shape(tile, tile),
            shape(tile, tile),
            shape(tile, cols),
        ],
        in_specs=in_vmem(1) + [pl.BlockSpec(memory_space=pl.ANY)],
        out_specs=in_vmem(6),
        scratch_shapes=[
            VMEM((span, width), F32),
            VMEM(lines.shape, F32),
            VMEM((tile, cols), F32),
            VMEM((row_count - 1, tile, cols), F32),
            VMEM((row_count, span, width), F32),
            VMEM((span, tile), F32),
            VMEM((row_count, span, tile), F32),
            VMEM((span, tile), F32),
            VMEM((count, span, tile), F32),
            VMEM((tile, 2 * tile), F32),
            DMA,
            DMA,
            DMA((row_count - 1,)),
            DMA((count - 1, tile_cols + 1)),
            DMA((count, tile_cols + 1)),
            *gather_sems(count),
            *gather_sems(count),
            *row_sems(row_count),
            *row_sems(row_count),
        ],
        compiler_params=params(0),
    )(own_lines, lines)


PARTS = 4


def product_kernel(
    row_count, count, groups, tile_cols,
    lines, panel_r, panel_c, top, inverse, mirror,
    out_r, out_c, update_r, update_c, reflector, out_mine,
    acc, near, mine, far, summed, full, picked, curve, slots, curve_total, curvature, work,
    nsend, nrecv, fsend, frecv, up_send, down_send, precv, *sems,
):
    row, col = lax.axis_index("row"), lax.axis_index("col")
    root, slot = lax.rem(col, row_count), col // row_count
    tile, width = panel_r.shape
    halves, _, sub, _ = acc.shape
    span = tile // count
    per = tile // PARTS // sub
    sibling, parity, half = sibling_of(col), lax.rem(col, 2), count // 2
    greet(others(row, row_count), others(col, count, 2) + [sibling])

    matrix, global_row, global_col = read_matrix(lines, width, tile, row_count, count, tile_cols)
    lower = jnp.where(global_row >= global_col, matrix, 0.0)
    acc[...] = dot3(panel_c[...], lower, NT).reshape(acc.shape)
    started = []

    def chunk_of(q):
        return q * halves // PARTS, (q * per) % count

    @pl.when(row == root)
    def _():
        for k in range(tile_cols):
            where = pl.ds(pl.multiple_of((k * groups + slot) * tile, tile), tile)
            value = mirror[:, k * tile : (k + 1) * tile].reshape(halves, count, sub, tile)
            acc[:, :, :, where] += value

    for h in range(halves):
        for k in range(half):
            j = 2 * k + 1 - parity
            started.append(
                copy_to("col", sibling, acc.at[h, j], near.at[h, k], nsend.at[h, k], nrecv.at[h, k])
            )
            started[-1].start()

    inv = inverse[...]
    out_r[...] = dot3(inv, panel_r[...], NN)
    vectors = out_r[...]
    block = dot(inv, top[...], NN) + unit(tile)
    factor = factor_steps(dot(block, block, TN), work)

    place = col // 2
    for h in range(halves):
        for k in range(half):
            copy_to(
                "col", sibling, acc.at[h, 0], near.at[h, k], nsend.at[h, k], nrecv.at[h, k]
            ).wait_recv()
            mine[h, k] = acc[h, 2 * k + parity] + near[h, k]
        for k, peer in enumerate(others(place, half)):
            started.append(
                copy_to(
                    "col", 2 * peer + parity, mine.at[h, peer], far.at[h, place], fsend.at[h, k],
                    frecv.at[h, place],
                )
            )
            started[-1].start()
    out_c[...] = dot3(inv, panel_c[...], NN)
    next(factor, None)

    gathers = [
        Gather(summed.at[h], full.at[h], sems[4 * h : 4 * h + 4], count) for h in range(halves)
    ]
    for h in range(halves):
        total = mine[h, place]
        for peer in others(place, half):
            copy_to(
                "col", 2 * peer + parity, mine.at[h, 0], far.at[h, peer], fsend.at[h, 0],
                frecv.at[h, peer],
            ).wait_recv()
            total = total + far[h, peer]
        summed[h] = total
        gathers[h].start()

    sems = sems[4 * halves :]
    curve[...] = dot3(summed[...].reshape(span, width), vectors, NT)
    curve_sum = RowSum(curve, slots, *sems[:2], row_count)
    curve_gather = Gather(curve_total, curvature, sems[2:6], count)
    curve_sum.start()
    next(factor, None)

    def pass_up(q):
        peer = jnp.minimum(row + 1, row_count - 1)
        return copy_to("row", peer, picked.at[q], picked.at[q], up_send.at[q], precv.at[q])

    def pass_down(q):
        peer = jnp.maximum(row - 1, 0)
        return copy_to("row", peer, picked.at[q], picked.at[q], down_send.at[q], precv.at[q])

    def pass_on(q, go, act):
        pl.when(go & (row >= root) & (row < row_count - 1))(lambda: act(pass_up(q)))
        pl.when(go & (row <= root) & (row > 0))(lambda: act(pass_down(q)))

    def pick(q):
        h, first = chunk_of(q)

        @pl.when(row == root)
        def _():
            for k in range(tile_cols):
                where = pl.ds(pl.multiple_of((k * groups + slot) * tile, tile), tile)
                value = full[h, first : first + per, :, where]
                picked[q, :, k * tile : (k + 1) * tile] = value.reshape(tile // PARTS, tile)

        pass_on(q, row == root, lambda copy: copy.start())

    for h in range(halves):
        gathers[h].finish()
        for q in range(h * PARTS // halves, (h + 1) * PARTS // halves):
            pick(q)
        if h == 0:
            curve_sum.finish()
            curve_total[...] = curve_sum.total()
            curve_gather.start()
    curve_gather.finish()
    for q in range(PARTS):
        pl.when(row > root)(lambda: pass_down(q).wait_recv())
        pl.when(row < root)(lambda: pass_up(q).wait_recv())
        pass_on(q, row != root, lambda copy: copy.start())
        if q in (0, PARTS - 1):
            next(factor, None)
    for _ in factor:
        pass

    inv2 = work[:, tile:]
    reflect = dot(inv2, dot(inv2, block, NT), TN)
    reflector[...] = reflect
    pieces = curvature[...]
    curvature_t = jnp.concatenate(
        [pieces[:, h * sub : (h + 1) * sub].reshape(tile // halves, tile) for h in range(halves)],
        axis=0,
    )
    both = dot(reflect, inv, TN)
    mixed = -0.5 * dot(dot(both, curvature_t, NN), reflect, NN)
    update_r[...] = dot3(both, full[...].reshape(tile, width), NN) + dot3(mixed, vectors, NN)
    update_c[...] = dot3(both, picked[...].reshape(tile, -1), NN) + dot3(mixed, out_c[...], NN)
    out_mine[...] = out_r[pl.ds(pl.multiple_of(col * span, span), span), :]

    for q in range(PARTS):
        pass_on(q, row >= 0, lambda copy: copy.wait_send())
    curve_sum.drain()
    for each in (*gathers, curve_gather):
        each.drain()
    for copy in started:
        copy.wait_send()


def read_matrix(lines, rows, tile, row_count, count, tile_cols):
    row, col = lax.axis_index("row"), lax.axis_index("col")
    strips = tile_cols * tile // 128
    matrix = jnp.concatenate(
        [lines[pl.ds(k, rows, stride=strips), :] for k in range(strips)], axis=1
    )
    r = lax.broadcasted_iota(jnp.int32, matrix.shape, 0)
    c = lax.broadcasted_iota(jnp.int32, matrix.shape, 1)
    global_row = (r // tile * row_count + row) * tile + r % tile
    global_col = (c // tile * count + col) * tile + c % tile
    return matrix, global_row, global_col


def product_step(lines, panel_r, panel_c, top, inverse, mirror, row_count, count, groups, tile_cols):
    tile, width = panel_r.shape
    cols = panel_c.shape[1]
    span, half = tile // count, count // 2
    halves = 2 if span % 16 == 0 else 1
    sub = span // halves
    part = (PARTS, tile // PARTS, cols)
    return pl.pallas_call(
        functools.partial(product_kernel, row_count, count, groups, tile_cols),
        out_shape=[
            shape(tile, width),
            shape(tile, cols),
            shape(tile, width),
            shape(tile, cols),
            shape(tile, tile),
            shape(span, width),
        ],
        in_specs=in_vmem(6),
        out_specs=in_vmem(6),
        scratch_shapes=[
            VMEM((halves, count, sub, width), F32),
            VMEM((halves, half, sub, width), F32),
            VMEM((halves, half, sub, width), F32),
            VMEM((halves, half, sub, width), F32),
            VMEM((halves, sub, width), F32),
            VMEM((halves, count, sub, width), F32),
            VMEM(part, F32),
            VMEM((span, tile), F32),
            VMEM((row_count, span, tile), F32),
            VMEM((span, tile), F32),
            VMEM((count, span, tile), F32),
            VMEM((tile, 2 * tile), F32),
            DMA((halves, half)),
            DMA((halves, half)),
            DMA((halves, half)),
            DMA((halves, half)),
            DMA((PARTS,)),
            DMA((PARTS,)),
            DMA((PARTS,)),
            *(gather_sems(count) * halves),
            *row_sems(row_count),
            *gather_sems(count),
        ],
        compiler_params=params(1),
    )(lines, panel_r, panel_c, top, inverse, mirror)


def update_kernel(
    row_count, count, tile_cols,
    where, lines, yr, xr, yc, xc, band, reflector, mine, out, out_band, out_reflector, out_mine,
):
    tile = yr.shape[0]
    strips = tile_cols * tile // 128
    step = pl.program_id(0)
    left = jnp.concatenate([yr[...], xr[...]], axis=0)
    right = jnp.concatenate([xc[...], yc[...]], axis=0)
    correction = dot3(left, right, TN)
    r = lax.broadcasted_iota(jnp.int32, (tile, 128), 0)
    c = lax.broadcasted_iota(jnp.int32, (tile, 128), 1)
    global_row = (step * row_count + where[0]) * tile + r
    for k in range(strips):
        first = (k * 128 // tile * count + where[1]) * tile + k * 128 % tile
        rows = pl.ds(k, tile, stride=strips)
        value = lines[rows, :] - correction[:, k * 128 : (k + 1) * 128]
        out[rows, :] = jnp.where(global_row >= first + c, value, 0.0)

    @pl.when(step == 0)
    def _():
        out_band[...] = band[...]
        out_reflector[...] = reflector[...]
        span, width = mine.shape
        for k in range(width // 128):
            rows = pl.ds(k, span, stride=width // 128)
            out_mine[rows, :] = mine[:, k * 128 : (k + 1) * 128]


def update_step(where, lines, yr, xr, yc, xc, rest, row_count, count, tile_cols):
    tile, width = yr.shape
    steps = width // tile
    block = (lines.shape[0] // steps, 128)
    strip = pl.BlockSpec((tile, tile), lambda i: (0, i))
    band, reflector, mine = rest
    mine_lines = shape(mine.size // 128, 128)

    def whole(array):
        return pl.BlockSpec(array.shape, lambda i: (0, 0))

    lined = pl.BlockSpec(block, lambda i: (i, 0))
    return pl.pallas_call(
        functools.partial(update_kernel, row_count, count, tile_cols),
        grid=(steps,),
        out_shape=[shape(*lines.shape), shape(tile, tile), shape(tile, tile), mine_lines],
        in_specs=[
            pl.BlockSpec(memory_space=pltpu.SMEM), lined, strip, strip, whole(yc), whole(xc),
            whole(band), whole(reflector), whole(mine),
        ],
        out_specs=[lined, whole(band), whole(reflector), whole(mine_lines)],
        compiler_params=params(),
    )(where, lines, yr, xr, yc, xc, band, reflector, mine)


def body(matrix, panel_t):
    tile_rows, _, tile, tile_cols = matrix.shape[:4]
    row_count, count = lax.axis_size("row"), lax.axis_size("col")
    groups = count // row_count
    span, width = tile // count, tile_rows * tile
    lines = matrix.reshape(-1, 128)
    sizes = (row_count, count, groups, tile_cols)
    panel_r, panel_c, top, band, inverse, mirror = panel_step(
        panel_t.reshape(-1, 128), lines, tile, *sizes
    )
    yr, yc, xr, xc, reflector, vectors = product_step(
        lines,
        panel_r.reshape(tile, width),
        panel_c.reshape(tile, -1),
        top.reshape(tile, tile),
        inverse,
        mirror,
        *sizes,
    )
    where = jnp.stack([lax.axis_index("row"), lax.axis_index("col")])
    updated, band, reflector, vectors = update_step(
        where, lines, yr, xr, yc, xc, (band, reflector, vectors), row_count, count, tile_cols
    )
    return (updated.reshape(matrix.shape), vectors.reshape(panel_t.shape), band, reflector)


def solution(mesh):
    placed = (P(None, "row", None, None, "col", None), P("col", None, "row", None))
    return jax.shard_map(
        body,
        mesh=mesh,
        in_specs=placed,
        out_specs=(P(None, "row", None, None, "col", None), P("col", None, "row", None), P(), P()),
        check_vma=False,
    )
```

```python
import functools

import jax
import jax.numpy as jnp
from jax import lax
from jax.experimental import pallas as pl
from jax.experimental.pallas import tpu as pltpu
from jax.sharding import PartitionSpec as P

F32 = jnp.float32
VMEM = pltpu.VMEM
HIGHEST = lax.Precision.HIGHEST
BLOCK = 64
GROUP = 4
HOOK = 16


def dot(a, b, over, precision=HIGHEST):
    return lax.dot_general(a, b, (over, ((), ())), precision=precision, preferred_element_type=F32)


NN = ((1,), (0,))
TN = ((0,), (0,))
NT = ((1,), (1,))


def in_vmem(count):
    return [pl.BlockSpec(memory_space=VMEM)] * count


def params(collective=None):
    if collective is None:
        return pltpu.CompilerParams(vmem_limit_bytes=48 << 20)
    return pltpu.CompilerParams(
        vmem_limit_bytes=48 << 20, collective_id=collective, has_side_effects=True
    )


def shape(*dims):
    return jax.ShapeDtypeStruct(dims, F32)


def inverse_steps(block):
    size = block.shape[0]
    row = lax.broadcasted_iota(jnp.int32, (size, 2 * size), 0)
    col = lax.broadcasted_iota(jnp.int32, (size, 2 * size), 1)
    work = jnp.concatenate([block, jnp.zeros_like(block)], axis=1)
    work = jnp.where(col == row + size, 1.0, work)
    scale = jnp.zeros((size, 2 * size), F32)
    for first in range(0, size, GROUP):
        if first % HOOK == 0:
            yield
        cols = [
            jnp.broadcast_to(work[:, first + t : first + t + 1], (size, 2 * size))
            for t in range(GROUP)
        ]
        for t in range(GROUP):
            j = first + t
            pivot = cols[t][j : j + 1, :]
            guess = pl.reciprocal(pivot, approx=True)
            factor = jnp.where(row > j, cols[t] * (guess * (2.0 - pivot * guess)), 0.0)
            for u in range(t + 1, GROUP):
                cols[u] = cols[u] - factor * cols[u][j : j + 1, :]
            work = work - factor * work[j : j + 1, :]
            scale = jnp.where(row == j, lax.rsqrt(pivot), scale)
    return (work * scale)[:, size:]


def dot3(a, b, over):
    ah, bh = a.astype(jnp.bfloat16), b.astype(jnp.bfloat16)
    al, bl = (a - ah.astype(F32)).astype(jnp.bfloat16), (b - bh.astype(F32)).astype(jnp.bfloat16)
    one = functools.partial(dot, over=over, precision=None)
    return one(ah, bl) + one(al, bh) + one(ah, bh)


def unit(size):
    row = lax.broadcasted_iota(jnp.int32, (size, size), 0)
    return (row == lax.broadcasted_iota(jnp.int32, (size, size), 1)).astype(F32)


def factor_steps(gram, work):
    size = gram.shape[0]
    work[:, :size] = gram
    work[:, size:] = unit(size)
    for lo in range(0, size, BLOCK):
        hi = lo + BLOCK
        inv = yield from inverse_steps(work[lo:hi, lo:hi])
        rows = dot(inv, work[lo:hi, :], NN)
        work[lo:hi, :] = rows
        if hi < size:
            work[hi:, :] -= dot(rows[:, hi:size], rows, TN)


def greet(row_peers, col_peers):
    barrier = pltpu.get_barrier_semaphore()
    for peer in row_peers:
        pl.semaphore_signal(
            barrier, inc=1, device_id={"row": peer}, device_id_type=pl.DeviceIdType.MESH
        )
    for peer in col_peers:
        pl.semaphore_signal(
            barrier, inc=1, device_id={"col": peer}, device_id_type=pl.DeviceIdType.MESH
        )
    pl.semaphore_wait(barrier, len(row_peers) + len(col_peers))


def copy_to(axis, peer, src, dst, send, recv):
    return pltpu.make_async_remote_copy(
        src_ref=src,
        dst_ref=dst,
        send_sem=send,
        recv_sem=recv,
        device_id={axis: peer},
        device_id_type=pl.DeviceIdType.MESH,
    )


def others(me, count, step=1):
    return [lax.rem(me + k, count) for k in range(step, count, step)]


def sibling_of(me):
    return me + 1 - 2 * lax.rem(me, 2)


class Gather:
    def __init__(self, src, out, sems, count):
        self.src, self.out, self.count = src, out, count
        self.near_send, self.near_recv, self.far_send, self.far_recv = sems
        self.me = lax.axis_index("col")
        self.sibling = sibling_of(self.me)
        self.started = []

    def near(self, src, slot):
        return copy_to(
            "col", self.sibling, src, self.out.at[slot], self.near_send.at[slot],
            self.near_recv.at[slot],
        )

    def far(self, peer, slot, k):
        return copy_to(
            "col", peer, self.src, self.out.at[slot], self.far_send.at[k], self.far_recv.at[slot]
        )

    def start(self):
        for k, peer in enumerate(others(self.me, self.count, 2)):
            self.started.append(self.far(peer, self.me, k))
            self.started[-1].start()
        self.started.append(self.near(self.src, self.me))
        self.started[-1].start()
        self.out[self.me] = self.src[...]

    def finish(self):
        for peer in others(self.me, self.count, 2):
            self.far(peer, peer, 0).wait_recv()
            self.started.append(self.near(self.out.at[peer], peer))
            self.started[-1].start()
        for k in range(0, self.count, 2):
            self.near(self.src, lax.rem(self.sibling + k, self.count)).wait_recv()

    def drain(self):
        for copy in self.started:
            copy.wait_send()


class RowSum:
    def __init__(self, src, slots, send, recv, count):
        self.src, self.slots, self.send, self.recv, self.count = src, slots, send, recv, count
        self.me = lax.axis_index("row")

    def copy(self, peer, slot, k):
        return copy_to(
            "row", peer, self.src, self.slots.at[slot], self.send.at[k], self.recv.at[slot]
        )

    def start(self):
        for k, peer in enumerate(others(self.me, self.count)):
            self.copy(peer, self.me, k).start()
        self.slots[self.me] = self.src[...]

    def finish(self):
        for peer in others(self.me, self.count):
            self.copy(peer, peer, 0).wait_recv()

    def total(self):
        total = self.slots[0]
        for k in range(1, self.count):
            total = total + self.slots[k]
        return total

    def drain(self):
        for k, peer in enumerate(others(self.me, self.count)):
            self.copy(peer, self.me, k).wait_send()


class RowRelay:
    def __init__(self, src, slots, up, down, recv, count):
        self.src, self.slots, self.sems, self.recv, self.count = src, slots, (up, down), recv, count
        self.me = lax.axis_index("row")

    def copy(self, slot, down):
        peer = jnp.maximum(self.me - 1, 0) if down else jnp.minimum(self.me + 1, self.count - 1)
        block = self.slots.at[slot]
        return copy_to("row", peer, block, block, self.sems[down].at[slot], self.recv.at[slot])

    def each(self, s, wait, act):
        me, last = self.me, self.count - 1
        for down in (0, 1):
            here = me + s <= last if down else me >= s
            there = me > 0 if down else me < last
            slot = jnp.minimum(me + s, last) if down else jnp.maximum(me - s, 0)
            if wait:
                pl.when(here)(lambda: self.copy(slot, down).wait_recv())
            pl.when(here & there)(lambda: act(self.copy(slot, down)))

    def start(self):
        self.slots[self.me] = self.src[...]
        self.each(0, False, lambda copy: copy.start())

    def step(self, s):
        self.each(s, True, lambda copy: copy.start())

    def drain(self):
        for s in range(self.count):
            self.each(s, False, lambda copy: copy.wait_send())


DMA = pltpu.SemaphoreType.DMA


def gather_sems(count):
    return [DMA((count,)), DMA((count,)), DMA((count // 2,)), DMA((count,))]


def row_sems(count):
    return [DMA((count - 1,)), DMA((count,))]


PARTS = 4


def panel_kernel(
    row_count, count, groups, tile_cols,
    own_hbm, lines_hbm, panel_r, panel_c, top, band, inverse, mirror_sum,
    mine, own_lines, lines, mirror, low, high, panel_z, part, slots, part_total, gram, work,
    load, chain_send, low_recv, high_recv, csend, crecv, *sems,
):
    row, col = lax.axis_index("row"), lax.axis_index("col")
    span, width = mine.shape
    tile = span * count
    peers = others(col, count)
    root = lax.rem(col, row_count)
    own_fetch = pltpu.make_async_copy(own_hbm, own_lines, load.at[0])
    own_fetch.start()
    fetch = pltpu.make_async_copy(lines_hbm, lines, load.at[1])
    fetch.start()
    greet(others(row, row_count), peers)
    own_fetch.wait()
    strips = width // 128
    for k in range(strips):
        mine[:, k * 128 : (k + 1) * 128] = own_lines[pl.ds(k, span, stride=strips), :]
    gather_r = Gather(mine, panel_r, sems[0:4], count)
    gather_g = Gather(part_total, gram, sems[4:8], count)
    rows_g = RowSum(part, slots, *sems[8:10], row_count)
    rows_z = RowRelay(mine, panel_z, *sems[10:13], row_count)
    gather_r.start()
    rows_z.start()
    gather_r.finish()
    part[...] = dot(mine[...], panel_r[...].reshape(tile, -1), NT)
    rows_g.start()
    rows_z.step(1)
    fetch.wait()
    matrix, global_row, global_col = read_matrix(lines, width, tile, row_count, count, tile_cols)
    strict = jnp.where(global_row > global_col, matrix, 0.0)
    products = dot3(panel_r[...].reshape(tile, width), strict, NN)
    mirror[...] = products.reshape(mirror.shape)
    if row_count > 2:
        rows_z.step(2)
    rows_g.finish()
    part_total[...] = rows_g.total()
    gather_g.start()

    depth = jnp.where(row > root, row_count - 1 - row, row)

    def hop_up(q):
        peer = jnp.minimum(row + 1, row_count - 1)
        return copy_to("row", peer, mirror.at[q], low.at[q], chain_send.at[q], low_recv.at[q])

    def hop_down(q):
        peer = jnp.maximum(row - 1, 0)
        return copy_to("row", peer, mirror.at[q], high.at[q], chain_send.at[q], high_recv.at[q])

    def hop(q, act):
        pl.when(row < root)(lambda: act(hop_up(q)))
        pl.when(row > root)(lambda: act(hop_down(q)))

    def take_low(q):
        peer = jnp.maximum(row - 1, 0)
        copy_to(
            "row", peer, mirror.at[q], low.at[q], chain_send.at[q], low_recv.at[q]
        ).wait_recv()
        mirror[q] += low[q]

    def take_high(q):
        peer = jnp.minimum(row + 1, row_count - 1)
        copy_to(
            "row", peer, mirror.at[q], high.at[q], chain_send.at[q], high_recv.at[q]
        ).wait_recv()
        mirror[q] += high[q]

    def relay(q):
        pl.when(row < root)(lambda: take_low(q))
        pl.when(row > root)(lambda: take_high(q))
        hop(q, lambda copy: copy.start())

    @pl.when((depth == 0) & (row != root))
    def _():
        for q in range(PARTS):
            hop(q, lambda copy: copy.start())

    for step in range(3, row_count):
        rows_z.step(step)
    gather_g.finish()

    def tiles_for(target):
        root, slot = lax.rem(target, row_count), target // row_count
        for k in range(tile_cols):
            start = pl.multiple_of((k * groups + slot) * tile, tile)
            yield panel_z.at[root, :, pl.ds(start, tile)], pl.ds(k * tile, tile)

    started = []
    for n, peer in enumerate(peers):
        for k, (src, at) in enumerate(tiles_for(peer)):
            started.append(
                copy_to("col", peer, src, panel_c.at[col, :, at], csend.at[n, k], crecv.at[col, k])
            )
        started.append(
            copy_to(
                "col", peer, panel_z.at[0, :, pl.ds(0, tile)], top.at[col],
                csend.at[n, tile_cols], crecv.at[col, tile_cols],
            )
        )
    for copy in started:
        copy.start()
    for src, at in tiles_for(col):
        panel_c[col, :, at] = src[...]
    top[col] = panel_z[0, :, :tile]

    def relays(due):
        for d in range(1, row_count - 1):
            for q in range(PARTS):
                if due(3 + 2 * q + 3 * (d - 1)):

                    @pl.when((depth == d) & (row != root))
                    def _():
                        relay(q)

    hooks = -1
    for hooks, _ in enumerate(factor_steps(gram[...].reshape(tile, tile), work)):
        relays(lambda at: at == hooks)
    relays(lambda at: at > hooks)
    keep = lax.broadcasted_iota(jnp.int32, (tile, tile), 1) >= lax.broadcasted_iota(
        jnp.int32, (tile, tile), 0
    )
    upper = jnp.where(keep, work[:, :tile], 0.0)
    band[...] = -upper
    inverse[...] = work[:, tile:]
    factor = upper.T
    for peer in peers:
        for k, (src, at) in enumerate(tiles_for(col)):
            copy_to(
                "col", peer, src, panel_c.at[peer, :, at], csend.at[0, k], crecv.at[peer, k]
            ).wait_recv()
        copy_to(
            "col", peer, top.at[col], top.at[peer], csend.at[0, 0], crecv.at[peer, tile_cols]
        ).wait_recv()
    for each in (gather_r, gather_g, rows_z, rows_g, *started):
        each.drain() if hasattr(each, "drain") else each.wait_send()

    @pl.when(row == 0)
    def _():
        panel_r[:, :, :tile] += factor.reshape(count, span, tile)

    @pl.when(col == 0)
    def _():
        panel_c[:, :, :tile] += factor.reshape(count, span, tile)

    for q in range(PARTS):
        hop(q, lambda copy: copy.wait_send())
        pl.when((row == root) & (row > 0))(lambda: take_low(q))
        pl.when((row == root) & (row < row_count - 1))(lambda: take_high(q))
    mirror_sum[...] = mirror[...].reshape(mirror_sum.shape)

    @pl.when((row == 0) & (col == 0))
    def _():
        mirror_sum[:, :tile] += dot3(factor, strict[:tile, :tile], NN)


def panel_step(own_lines, lines, tile, row_count, count, groups, tile_cols):
    span = tile // count
    width = own_lines.shape[0] * 128 // span
    cols = tile_cols * tile
    return pl.pallas_call(
        functools.partial(panel_kernel, row_count, count, groups, tile_cols),
        out_shape=[
            shape(count, span, width),
            shape(count, span, tile_cols * tile),
            shape(count, span, tile),
            shape(tile, tile),
            shape(tile, tile),
            shape(tile, cols),
        ],
        in_specs=[pl.BlockSpec(memory_space=pltpu.HBM)] * 2,
        out_specs=in_vmem(6),
        scratch_shapes=[
            VMEM((span, width), F32),
            VMEM(own_lines.shape, F32),
            VMEM(lines.shape, F32),
            VMEM((PARTS, tile // PARTS, cols), F32),
            VMEM((PARTS, tile // PARTS, cols), F32),
            VMEM((PARTS, tile // PARTS, cols), F32),
            VMEM((row_count, span, width), F32),
            VMEM((span, tile), F32),
            VMEM((row_count, span, tile), F32),
            VMEM((span, tile), F32),
            VMEM((count, span, tile), F32),
            VMEM((tile, 2 * tile), F32),
            DMA((2,)),
            DMA((PARTS,)),
            DMA((PARTS,)),
            DMA((PARTS,)),
            DMA((count - 1, tile_cols + 1)),
            DMA((count, tile_cols + 1)),
            *gather_sems(count),
            *gather_sems(count),
            *row_sems(row_count),
            DMA((row_count,)),
            DMA((row_count,)),
            DMA((row_count,)),
        ],
        compiler_params=params(0),
    )(own_lines, lines)


def product_kernel(
    row_count, count, groups, tile_cols,
    lines, panel_r, panel_c, top, inverse, mirror,
    out_r, out_c, update_r, update_c, reflector, out_mine,
    acc, near, mine, far, summed, full, picked, curve, slots, curve_total, curvature, work,
    nsend, nrecv, fsend, frecv, up_send, down_send, precv, *sems,
):
    row, col = lax.axis_index("row"), lax.axis_index("col")
    root, slot = lax.rem(col, row_count), col // row_count
    tile, width = panel_r.shape
    halves, _, sub, _ = acc.shape
    span = tile // count
    per = tile // PARTS // sub
    sibling, parity, half = sibling_of(col), lax.rem(col, 2), count // 2
    greet(others(row, row_count), others(col, count, 2) + [sibling])

    matrix, global_row, global_col = read_matrix(lines, width, tile, row_count, count, tile_cols)
    lower = jnp.where(global_row >= global_col, matrix, 0.0)
    acc[...] = dot3(panel_c[...], lower, NT).reshape(acc.shape)
    started = []

    def chunk_of(q):
        return q * halves // PARTS, (q * per) % count

    @pl.when(row == root)
    def _():
        for k in range(tile_cols):
            where = pl.ds(pl.multiple_of((k * groups + slot) * tile, tile), tile)
            value = mirror[:, k * tile : (k + 1) * tile].reshape(halves, count, sub, tile)
            acc[:, :, :, where] += value

    for h in range(halves):
        for k in range(half):
            j = 2 * k + 1 - parity
            started.append(
                copy_to("col", sibling, acc.at[h, j], near.at[h, k], nsend.at[h, k], nrecv.at[h, k])
            )
            started[-1].start()

    inv = inverse[...]
    out_r[...] = dot3(inv, panel_r[...], NN)
    vectors = out_r[...]
    block = dot(inv, top[...], NN) + unit(tile)
    factor = factor_steps(dot(block, block, TN), work)

    place = col // 2
    for h in range(halves):
        for k in range(half):
            copy_to(
                "col", sibling, acc.at[h, 0], near.at[h, k], nsend.at[h, k], nrecv.at[h, k]
            ).wait_recv()
            mine[h, k] = acc[h, 2 * k + parity] + near[h, k]
        for k, peer in enumerate(others(place, half)):
            started.append(
                copy_to(
                    "col", 2 * peer + parity, mine.at[h, peer], far.at[h, place], fsend.at[h, k],
                    frecv.at[h, place],
                )
            )
            started[-1].start()
    out_c[...] = dot3(inv, panel_c[...], NN)
    for _ in range(4):
        next(factor, None)

    gathers = [
        Gather(summed.at[h], full.at[h], sems[4 * h : 4 * h + 4], count) for h in range(halves)
    ]
    for h in range(halves):
        total = mine[h, place]
        for peer in others(place, half):
            copy_to(
                "col", 2 * peer + parity, mine.at[h, 0], far.at[h, peer], fsend.at[h, 0],
                frecv.at[h, peer],
            ).wait_recv()
            total = total + far[h, peer]
        summed[h] = total
        gathers[h].start()

    sems = sems[4 * halves :]
    curve[...] = dot3(summed[...].reshape(span, width), vectors, NT)
    curve_sum = RowSum(curve, slots, *sems[:2], row_count)
    curve_gather = Gather(curve_total, curvature, sems[2:6], count)
    curve_sum.start()

    def pass_up(q):
        peer = jnp.minimum(row + 1, row_count - 1)
        return copy_to("row", peer, picked.at[q], picked.at[q], up_send.at[q], precv.at[q])

    def pass_down(q):
        peer = jnp.maximum(row - 1, 0)
        return copy_to("row", peer, picked.at[q], picked.at[q], down_send.at[q], precv.at[q])

    def pass_on(q, go, act):
        pl.when(go & (row >= root) & (row < row_count - 1))(lambda: act(pass_up(q)))
        pl.when(go & (row <= root) & (row > 0))(lambda: act(pass_down(q)))

    def pick(q):
        h, first = chunk_of(q)

        @pl.when(row == root)
        def _():
            for k in range(tile_cols):
                where = pl.ds(pl.multiple_of((k * groups + slot) * tile, tile), tile)
                value = full[h, first : first + per, :, where]
                picked[q, :, k * tile : (k + 1) * tile] = value.reshape(tile // PARTS, tile)

        pass_on(q, row == root, lambda copy: copy.start())

    for h in range(halves):
        gathers[h].finish()
        for q in range(h * PARTS // halves, (h + 1) * PARTS // halves):
            pick(q)
        if h == 0:
            curve_sum.finish()
            curve_total[...] = curve_sum.total()
            curve_gather.start()
    away = jnp.where(row > root, row - root, root - row)
    at_end = (row == 0) | (row == row_count - 1)

    def arrive(q):
        pl.when(row > root)(lambda: pass_down(q).wait_recv())
        pl.when(row < root)(lambda: pass_up(q).wait_recv())

    def relays(due):
        for d in range(1, row_count - 1):
            for q in range(PARTS):
                if due(2 * q + 2 * (d - 1)):

                    @pl.when((away == d) & jnp.logical_not(at_end))
                    def _():
                        arrive(q)
                        pass_on(q, row != root, lambda copy: copy.start())

    hooks = -1
    for hooks, _ in enumerate(factor):
        relays(lambda at: at == hooks)
        if hooks == 1:
            curve_gather.finish()
    relays(lambda at: at > hooks)
    inv2 = work[:, tile:]
    reflect = dot(inv2, dot(inv2, block, NT), TN)
    reflector[...] = reflect
    pieces = curvature[...]
    curvature_t = jnp.concatenate(
        [pieces[:, h * sub : (h + 1) * sub].reshape(tile // halves, tile) for h in range(halves)],
        axis=0,
    )
    both = dot(reflect, inv, TN)
    mixed = -0.5 * dot(dot(both, curvature_t, NN), reflect, NN)
    update_r[...] = dot3(both, full[...].reshape(tile, width), NN) + dot3(mixed, vectors, NN)
    for q in range(PARTS):
        pl.when(at_end)(lambda: arrive(q))
    update_c[...] = dot3(both, picked[...].reshape(tile, -1), NN) + dot3(mixed, out_c[...], NN)
    out_mine[...] = out_r[pl.ds(pl.multiple_of(col * span, span), span), :]

    for q in range(PARTS):
        pass_on(q, row >= 0, lambda copy: copy.wait_send())
    curve_sum.drain()
    for each in (*gathers, curve_gather):
        each.drain()
    for copy in started:
        copy.wait_send()


def read_matrix(lines, rows, tile, row_count, count, tile_cols):
    row, col = lax.axis_index("row"), lax.axis_index("col")
    strips = tile_cols * tile // 128
    matrix = jnp.concatenate(
        [lines[pl.ds(k, rows, stride=strips), :] for k in range(strips)], axis=1
    )
    r = lax.broadcasted_iota(jnp.int32, matrix.shape, 0)
    c = lax.broadcasted_iota(jnp.int32, matrix.shape, 1)
    global_row = (r // tile * row_count + row) * tile + r % tile
    global_col = (c // tile * count + col) * tile + c % tile
    return matrix, global_row, global_col


def product_step(lines, panel_r, panel_c, top, inverse, mirror, row_count, count, groups, tile_cols):
    tile, width = panel_r.shape
    cols = panel_c.shape[1]
    span, half = tile // count, count // 2
    halves = 4 if span % 32 == 0 else 1
    sub = span // halves
    part = (PARTS, tile // PARTS, cols)
    return pl.pallas_call(
        functools.partial(product_kernel, row_count, count, groups, tile_cols),
        out_shape=[
            shape(tile, width),
            shape(tile, cols),
            shape(tile, width),
            shape(tile, cols),
            shape(tile, tile),
            shape(span, width),
        ],
        in_specs=in_vmem(6),
        out_specs=in_vmem(6),
        scratch_shapes=[
            VMEM((halves, count, sub, width), F32),
            VMEM((halves, half, sub, width), F32),
            VMEM((halves, half, sub, width), F32),
            VMEM((halves, half, sub, width), F32),
            VMEM((halves, sub, width), F32),
            VMEM((halves, count, sub, width), F32),
            VMEM(part, F32),
            VMEM((span, tile), F32),
            VMEM((row_count, span, tile), F32),
            VMEM((span, tile), F32),
            VMEM((count, span, tile), F32),
            VMEM((tile, 2 * tile), F32),
            DMA((halves, half)),
            DMA((halves, half)),
            DMA((halves, half)),
            DMA((halves, half)),
            DMA((PARTS,)),
            DMA((PARTS,)),
            DMA((PARTS,)),
            *(gather_sems(count) * halves),
            *row_sems(row_count),
            *gather_sems(count),
        ],
        compiler_params=params(1),
    )(lines, panel_r, panel_c, top, inverse, mirror)


def update_kernel(
    row_count, count, tile_cols,
    where, lines, yr, xr, yc, xc, band, reflector, mine, out, out_band, out_reflector, out_mine,
):
    tile = yr.shape[0]
    strips = tile_cols * tile // 128
    step = pl.program_id(0)
    left = jnp.concatenate([yr[...], xr[...]], axis=0)
    right = jnp.concatenate([xc[...], yc[...]], axis=0)
    correction = dot3(left, right, TN)
    r = lax.broadcasted_iota(jnp.int32, (tile, 128), 0)
    c = lax.broadcasted_iota(jnp.int32, (tile, 128), 1)
    global_row = (step * row_count + where[0]) * tile + r
    for k in range(strips):
        first = (k * 128 // tile * count + where[1]) * tile + k * 128 % tile
        rows = pl.ds(k, tile, stride=strips)
        value = lines[rows, :] - correction[:, k * 128 : (k + 1) * 128]
        out[rows, :] = jnp.where(global_row >= first + c, value, 0.0)

    @pl.when(step == 0)
    def _():
        out_band[...] = band[...]
        out_reflector[...] = reflector[...]
        span, width = mine.shape
        for k in range(width // 128):
            rows = pl.ds(k, span, stride=width // 128)
            out_mine[rows, :] = mine[:, k * 128 : (k + 1) * 128]


def update_step(where, lines, yr, xr, yc, xc, rest, row_count, count, tile_cols):
    tile, width = yr.shape
    steps = width // tile
    block = (lines.shape[0] // steps, 128)
    strip = pl.BlockSpec((tile, tile), lambda i: (0, i))
    band, reflector, mine = rest
    mine_lines = shape(mine.size // 128, 128)

    def whole(array):
        return pl.BlockSpec(array.shape, lambda i: (0, 0))

    lined = pl.BlockSpec(block, lambda i: (i, 0))
    return pl.pallas_call(
        functools.partial(update_kernel, row_count, count, tile_cols),
        grid=(steps,),
        out_shape=[shape(*lines.shape), shape(tile, tile), shape(tile, tile), mine_lines],
        in_specs=[
            pl.BlockSpec(memory_space=pltpu.SMEM), lined, strip, strip, whole(yc), whole(xc),
            whole(band), whole(reflector), whole(mine),
        ],
        out_specs=[lined, whole(band), whole(reflector), whole(mine_lines)],
        compiler_params=params(),
    )(where, lines, yr, xr, yc, xc, band, reflector, mine)


def body(matrix, panel_t):
    tile_rows, _, tile, tile_cols = matrix.shape[:4]
    row_count, count = lax.axis_size("row"), lax.axis_size("col")
    groups = count // row_count
    span, width = tile // count, tile_rows * tile
    lines = matrix.reshape(-1, 128)
    sizes = (row_count, count, groups, tile_cols)
    panel_r, panel_c, top, band, inverse, mirror = panel_step(
        panel_t.reshape(-1, 128), lines, tile, *sizes
    )
    yr, yc, xr, xc, reflector, vectors = product_step(
        lines,
        panel_r.reshape(tile, width),
        panel_c.reshape(tile, -1),
        top.reshape(tile, tile),
        inverse,
        mirror,
        *sizes,
    )
    where = jnp.stack([lax.axis_index("row"), lax.axis_index("col")])
    updated, band, reflector, vectors = update_step(
        where, lines, yr, xr, yc, xc, (band, reflector, vectors), row_count, count, tile_cols
    )
    return (updated.reshape(matrix.shape), vectors.reshape(panel_t.shape), band, reflector)


def solution(mesh):
    placed = (P(None, "row", None, None, "col", None), P("col", None, "row", None))
    return jax.shard_map(
        body,
        mesh=mesh,
        in_specs=placed,
        out_specs=(P(None, "row", None, None, "col", None), P("col", None, "row", None), P(), P()),
        check_vma=False,
    )
```

```python
import functools

import jax
import jax.numpy as jnp
from jax import lax
from jax.experimental import pallas as pl
from jax.experimental.pallas import tpu as pltpu
from jax.sharding import PartitionSpec as P

F32 = jnp.float32
VMEM = pltpu.VMEM
HIGHEST = lax.Precision.HIGHEST
BLOCK = 64
GROUP = 8
HOOK = 16


def dot(a, b, over, precision=HIGHEST):
    return lax.dot_general(a, b, (over, ((), ())), precision=precision, preferred_element_type=F32)


NN = ((1,), (0,))
TN = ((0,), (0,))
NT = ((1,), (1,))


def in_vmem(count):
    return [pl.BlockSpec(memory_space=VMEM)] * count


def params(collective=None):
    if collective is None:
        return pltpu.CompilerParams(vmem_limit_bytes=48 << 20)
    return pltpu.CompilerParams(
        vmem_limit_bytes=48 << 20, collective_id=collective, has_side_effects=True
    )


def shape(*dims):
    return jax.ShapeDtypeStruct(dims, F32)


def inverse_steps(block):
    size = block.shape[0]
    wide = (GROUP, 2 * size)
    sub = lax.broadcasted_iota(jnp.int32, wide, 0)
    lane = lax.broadcasted_iota(jnp.int32, wide, 1)
    count = size // GROUP
    work, scales = [], []
    for g in range(count):
        rows = block[g * GROUP : (g + 1) * GROUP, :]
        rows = jnp.concatenate([rows, jnp.zeros_like(rows)], axis=1)
        work.append(jnp.where(lane == sub + (g * GROUP + size), 1.0, rows))
    for g in range(count):
        if g * GROUP % HOOK == 0:
            yield
        first = g * GROUP
        cols = {
            r: [
                jnp.broadcast_to(work[r][:, first + t : first + t + 1], wide)
                for t in range(GROUP)
            ]
            for r in range(g, count)
        }
        pivot = [[cols[g][b][a : a + 1, :] for b in range(GROUP)] for a in range(GROUP)]
        row = [work[g][a : a + 1, :] for a in range(GROUP)]
        inverse = []
        scale = jnp.zeros(wide, F32)
        for t in range(GROUP):
            guess = pl.reciprocal(pivot[t][t], approx=True)
            inverse.append(guess * (2.0 - pivot[t][t] * guess))
            scale = jnp.where(sub == t, lax.rsqrt(pivot[t][t]), scale)
            for a in range(t + 1, GROUP):
                factor = pivot[a][t] * inverse[t]
                for b in range(t + 1, GROUP):
                    pivot[a][b] = pivot[a][b] - factor * pivot[t][b]
                row[a] = row[a] - factor * row[t]
        scales.append(scale)
        for r in range(g, count):
            factors = []
            for t in range(GROUP):
                value = cols[r][t]
                for s in range(t):
                    value = value - factors[s] * pivot[s][t]
                value = value * inverse[t]
                factors.append(jnp.where(sub > t, value, 0.0) if r == g else value)
            total = work[r]
            for t in range(GROUP):
                total = total - factors[t] * row[t]
            work[r] = total
    return jnp.concatenate([work[g] * scales[g] for g in range(count)], axis=0)[:, size:]


def dot3(a, b, over):
    ah, bh = a.astype(jnp.bfloat16), b.astype(jnp.bfloat16)
    al, bl = (a - ah.astype(F32)).astype(jnp.bfloat16), (b - bh.astype(F32)).astype(jnp.bfloat16)
    one = functools.partial(dot, over=over, precision=None)
    return one(ah, bl) + one(al, bh) + one(ah, bh)


def unit(size):
    row = lax.broadcasted_iota(jnp.int32, (size, size), 0)
    return (row == lax.broadcasted_iota(jnp.int32, (size, size), 1)).astype(F32)


def factor_steps(gram, work):
    size = gram.shape[0]
    work[:, :size] = gram
    work[:, size:] = unit(size)
    for lo in range(0, size, BLOCK):
        hi = lo + BLOCK
        inv = yield from inverse_steps(work[lo:hi, lo:hi])
        rows = dot(inv, work[lo:hi, :], NN)
        work[lo:hi, :] = rows
        if hi < size:
            work[hi:, :] -= dot(rows[:, hi:size], rows, TN)


def greet(row_peers, col_peers):
    barrier = pltpu.get_barrier_semaphore()
    for peer in row_peers:
        pl.semaphore_signal(
            barrier, inc=1, device_id={"row": peer}, device_id_type=pl.DeviceIdType.MESH
        )
    for peer in col_peers:
        pl.semaphore_signal(
            barrier, inc=1, device_id={"col": peer}, device_id_type=pl.DeviceIdType.MESH
        )
    pl.semaphore_wait(barrier, len(row_peers) + len(col_peers))


def copy_to(axis, peer, src, dst, send, recv):
    return pltpu.make_async_remote_copy(
        src_ref=src,
        dst_ref=dst,
        send_sem=send,
        recv_sem=recv,
        device_id={axis: peer},
        device_id_type=pl.DeviceIdType.MESH,
    )


def others(me, count, step=1):
    return [lax.rem(me + k, count) for k in range(step, count, step)]


def sibling_of(me):
    return me + 1 - 2 * lax.rem(me, 2)


class Gather:
    def __init__(self, src, out, sems, count):
        self.src, self.out, self.count = src, out, count
        self.near_send, self.near_recv, self.far_send, self.far_recv = sems
        self.me = lax.axis_index("col")
        self.sibling = sibling_of(self.me)
        self.started = []

    def near(self, src, slot):
        return copy_to(
            "col", self.sibling, src, self.out.at[slot], self.near_send.at[slot],
            self.near_recv.at[slot],
        )

    def far(self, peer, slot, k):
        return copy_to(
            "col", peer, self.src, self.out.at[slot], self.far_send.at[k], self.far_recv.at[slot]
        )

    def start(self):
        for k, peer in enumerate(others(self.me, self.count, 2)):
            self.started.append(self.far(peer, self.me, k))
            self.started[-1].start()
        self.started.append(self.near(self.src, self.me))
        self.started[-1].start()
        self.out[self.me] = self.src[...]

    def finish(self):
        for peer in others(self.me, self.count, 2):
            self.far(peer, peer, 0).wait_recv()
            self.started.append(self.near(self.out.at[peer], peer))
            self.started[-1].start()
        for k in range(0, self.count, 2):
            self.near(self.src, lax.rem(self.sibling + k, self.count)).wait_recv()

    def drain(self):
        for copy in self.started:
            copy.wait_send()


class RowSum:
    def __init__(self, src, slots, send, recv, count):
        self.src, self.slots, self.send, self.recv, self.count = src, slots, send, recv, count
        self.me = lax.axis_index("row")

    def copy(self, peer, slot, k):
        return copy_to(
            "row", peer, self.src, self.slots.at[slot], self.send.at[k], self.recv.at[slot]
        )

    def start(self):
        for k, peer in enumerate(others(self.me, self.count)):
            self.copy(peer, self.me, k).start()
        self.slots[self.me] = self.src[...]

    def finish(self):
        for peer in others(self.me, self.count):
            self.copy(peer, peer, 0).wait_recv()

    def total(self):
        total = self.slots[0]
        for k in range(1, self.count):
            total = total + self.slots[k]
        return total

    def drain(self):
        for k, peer in enumerate(others(self.me, self.count)):
            self.copy(peer, self.me, k).wait_send()


class RowRelay:
    def __init__(self, src, slots, up, down, recv, count):
        self.src, self.slots, self.sems, self.recv, self.count = src, slots, (up, down), recv, count
        self.me = lax.axis_index("row")

    def copy(self, slot, down):
        peer = jnp.maximum(self.me - 1, 0) if down else jnp.minimum(self.me + 1, self.count - 1)
        block = self.slots.at[slot]
        return copy_to("row", peer, block, block, self.sems[down].at[slot], self.recv.at[slot])

    def each(self, s, wait, act):
        me, last = self.me, self.count - 1
        for down in (0, 1):
            here = me + s <= last if down else me >= s
            there = me > 0 if down else me < last
            slot = jnp.minimum(me + s, last) if down else jnp.maximum(me - s, 0)
            if wait:
                pl.when(here)(lambda: self.copy(slot, down).wait_recv())
            pl.when(here & there)(lambda: act(self.copy(slot, down)))

    def start(self):
        self.slots[self.me] = self.src[...]
        self.each(0, False, lambda copy: copy.start())

    def step(self, s):
        self.each(s, True, lambda copy: copy.start())

    def drain(self):
        for s in range(self.count):
            self.each(s, False, lambda copy: copy.wait_send())


DMA = pltpu.SemaphoreType.DMA


def gather_sems(count):
    return [DMA((count,)), DMA((count,)), DMA((count // 2,)), DMA((count,))]


def row_sems(count):
    return [DMA((count - 1,)), DMA((count,))]


PARTS = 4


def panel_kernel(
    row_count, count, groups, tile_cols,
    own_hbm, lines_hbm, panel_r, panel_c, top, band, inverse, mirror_sum,
    mine, own_lines, lines, mirror, low, high, panel_z, part, slots, part_total, gram, work,
    load, chain_send, low_recv, high_recv, csend, crecv, *sems,
):
    row, col = lax.axis_index("row"), lax.axis_index("col")
    span, width = mine.shape
    tile = span * count
    peers = others(col, count)
    root = lax.rem(col, row_count)
    own_fetch = pltpu.make_async_copy(own_hbm, own_lines, load.at[0])
    own_fetch.start()
    fetch = pltpu.make_async_copy(lines_hbm, lines, load.at[1])
    fetch.start()
    greet(others(row, row_count), peers)
    own_fetch.wait()
    strips = width // 128
    for k in range(strips):
        mine[:, k * 128 : (k + 1) * 128] = own_lines[pl.ds(k, span, stride=strips), :]
    gather_r = Gather(mine, panel_r, sems[0:4], count)
    gather_g = Gather(part_total, gram, sems[4:8], count)
    rows_g = RowSum(part, slots, *sems[8:10], row_count)
    rows_z = RowRelay(mine, panel_z, *sems[10:13], row_count)
    gather_r.start()
    rows_z.start()
    gather_r.finish()
    part[...] = dot(mine[...], panel_r[...].reshape(tile, -1), NT)
    rows_g.start()
    rows_z.step(1)
    fetch.wait()
    matrix, global_row, global_col = read_matrix(lines, width, tile, row_count, count, tile_cols)
    strict = jnp.where(global_row > global_col, matrix, 0.0)
    products = dot3(panel_r[...].reshape(tile, width), strict, NN)
    mirror[...] = products.reshape(mirror.shape)
    if row_count > 2:
        rows_z.step(2)
    rows_g.finish()
    part_total[...] = rows_g.total()
    gather_g.start()

    depth = jnp.where(row > root, row_count - 1 - row, row)

    def hop_up(q):
        peer = jnp.minimum(row + 1, row_count - 1)
        return copy_to("row", peer, mirror.at[q], low.at[q], chain_send.at[q], low_recv.at[q])

    def hop_down(q):
        peer = jnp.maximum(row - 1, 0)
        return copy_to("row", peer, mirror.at[q], high.at[q], chain_send.at[q], high_recv.at[q])

    def hop(q, act):
        pl.when(row < root)(lambda: act(hop_up(q)))
        pl.when(row > root)(lambda: act(hop_down(q)))

    def take_low(q):
        peer = jnp.maximum(row - 1, 0)
        copy_to(
            "row", peer, mirror.at[q], low.at[q], chain_send.at[q], low_recv.at[q]
        ).wait_recv()
        mirror[q] += low[q]

    def take_high(q):
        peer = jnp.minimum(row + 1, row_count - 1)
        copy_to(
            "row", peer, mirror.at[q], high.at[q], chain_send.at[q], high_recv.at[q]
        ).wait_recv()
        mirror[q] += high[q]

    def relay(q):
        pl.when(row < root)(lambda: take_low(q))
        pl.when(row > root)(lambda: take_high(q))
        hop(q, lambda copy: copy.start())

    @pl.when((depth == 0) & (row != root))
    def _():
        for q in range(PARTS):
            hop(q, lambda copy: copy.start())

    for step in range(3, row_count):
        rows_z.step(step)
    gather_g.finish()

    def tiles_for(target):
        root, slot = lax.rem(target, row_count), target // row_count
        for k in range(tile_cols):
            start = pl.multiple_of((k * groups + slot) * tile, tile)
            yield panel_z.at[root, :, pl.ds(start, tile)], pl.ds(k * tile, tile)

    started = []
    for n, peer in enumerate(peers):
        for k, (src, at) in enumerate(tiles_for(peer)):
            started.append(
                copy_to("col", peer, src, panel_c.at[col, :, at], csend.at[n, k], crecv.at[col, k])
            )
        started.append(
            copy_to(
                "col", peer, panel_z.at[0, :, pl.ds(0, tile)], top.at[col],
                csend.at[n, tile_cols], crecv.at[col, tile_cols],
            )
        )
    for copy in started:
        copy.start()
    for src, at in tiles_for(col):
        panel_c[col, :, at] = src[...]
    top[col] = panel_z[0, :, :tile]

    def relays(due):
        for d in range(1, row_count - 1):
            for q in range(PARTS):
                if due(3 + 2 * q + 3 * (d - 1)):

                    @pl.when((depth == d) & (row != root))
                    def _():
                        relay(q)

    hooks = -1
    for hooks, _ in enumerate(factor_steps(gram[...].reshape(tile, tile), work)):
        relays(lambda at: at == hooks)
    relays(lambda at: at > hooks)
    keep = lax.broadcasted_iota(jnp.int32, (tile, tile), 1) >= lax.broadcasted_iota(
        jnp.int32, (tile, tile), 0
    )
    upper = jnp.where(keep, work[:, :tile], 0.0)
    band[...] = -upper
    inverse[...] = work[:, tile:]
    factor = upper.T
    for peer in peers:
        for k, (src, at) in enumerate(tiles_for(col)):
            copy_to(
                "col", peer, src, panel_c.at[peer, :, at], csend.at[0, k], crecv.at[peer, k]
            ).wait_recv()
        copy_to(
            "col", peer, top.at[col], top.at[peer], csend.at[0, 0], crecv.at[peer, tile_cols]
        ).wait_recv()
    for each in (gather_r, gather_g, rows_z, rows_g, *started):
        each.drain() if hasattr(each, "drain") else each.wait_send()

    @pl.when(row == 0)
    def _():
        panel_r[:, :, :tile] += factor.reshape(count, span, tile)

    @pl.when(col == 0)
    def _():
        panel_c[:, :, :tile] += factor.reshape(count, span, tile)

    for q in range(PARTS):
        hop(q, lambda copy: copy.wait_send())
        pl.when((row == root) & (row > 0))(lambda: take_low(q))
        pl.when((row == root) & (row < row_count - 1))(lambda: take_high(q))
    mirror_sum[...] = mirror[...].reshape(mirror_sum.shape)

    @pl.when((row == 0) & (col == 0))
    def _():
        mirror_sum[:, :tile] += dot3(factor, strict[:tile, :tile], NN)


def panel_step(own_lines, lines, tile, row_count, count, groups, tile_cols):
    span = tile // count
    width = own_lines.shape[0] * 128 // span
    cols = tile_cols * tile
    return pl.pallas_call(
        functools.partial(panel_kernel, row_count, count, groups, tile_cols),
        out_shape=[
            shape(count, span, width),
            shape(count, span, tile_cols * tile),
            shape(count, span, tile),
            shape(tile, tile),
            shape(tile, tile),
            shape(tile, cols),
        ],
        in_specs=[pl.BlockSpec(memory_space=pltpu.HBM)] * 2,
        out_specs=in_vmem(6),
        scratch_shapes=[
            VMEM((span, width), F32),
            VMEM(own_lines.shape, F32),
            VMEM(lines.shape, F32),
            VMEM((PARTS, tile // PARTS, cols), F32),
            VMEM((PARTS, tile // PARTS, cols), F32),
            VMEM((PARTS, tile // PARTS, cols), F32),
            VMEM((row_count, span, width), F32),
            VMEM((span, tile), F32),
            VMEM((row_count, span, tile), F32),
            VMEM((span, tile), F32),
            VMEM((count, span, tile), F32),
            VMEM((tile, 2 * tile), F32),
            DMA((2,)),
            DMA((PARTS,)),
            DMA((PARTS,)),
            DMA((PARTS,)),
            DMA((count - 1, tile_cols + 1)),
            DMA((count, tile_cols + 1)),
            *gather_sems(count),
            *gather_sems(count),
            *row_sems(row_count),
            DMA((row_count,)),
            DMA((row_count,)),
            DMA((row_count,)),
        ],
        compiler_params=params(0),
    )(own_lines, lines)


def product_kernel(
    row_count, count, groups, tile_cols,
    lines, panel_r, panel_c, top, inverse, mirror,
    out_r, out_c, update_r, update_c, reflector, out_mine,
    acc, near, mine, far, summed, full, picked, curve, slots, curve_total, curvature, work,
    nsend, nrecv, fsend, frecv, up_send, down_send, precv, *sems,
):
    row, col = lax.axis_index("row"), lax.axis_index("col")
    root, slot = lax.rem(col, row_count), col // row_count
    tile, width = panel_r.shape
    halves, _, sub, _ = acc.shape
    span = tile // count
    per = tile // PARTS // sub
    sibling, parity, half = sibling_of(col), lax.rem(col, 2), count // 2
    greet(others(row, row_count), others(col, count, 2) + [sibling])

    matrix, global_row, global_col = read_matrix(lines, width, tile, row_count, count, tile_cols)
    lower = jnp.where(global_row >= global_col, matrix, 0.0)
    acc[...] = dot3(panel_c[...], lower, NT).reshape(acc.shape)
    started = []

    def chunk_of(q):
        return q * halves // PARTS, (q * per) % count

    @pl.when(row == root)
    def _():
        for k in range(tile_cols):
            where = pl.ds(pl.multiple_of((k * groups + slot) * tile, tile), tile)
            value = mirror[:, k * tile : (k + 1) * tile].reshape(halves, count, sub, tile)
            acc[:, :, :, where] += value

    for h in range(halves):
        for k in range(half):
            j = 2 * k + 1 - parity
            started.append(
                copy_to("col", sibling, acc.at[h, j], near.at[h, k], nsend.at[h, k], nrecv.at[h, k])
            )
            started[-1].start()

    inv = inverse[...]
    out_r[...] = dot3(inv, panel_r[...], NN)
    vectors = out_r[...]
    block = dot(inv, top[...], NN) + unit(tile)
    factor = factor_steps(dot(block, block, TN), work)

    place = col // 2
    for h in range(halves):
        for k in range(half):
            copy_to(
                "col", sibling, acc.at[h, 0], near.at[h, k], nsend.at[h, k], nrecv.at[h, k]
            ).wait_recv()
            mine[h, k] = acc[h, 2 * k + parity] + near[h, k]
        for k, peer in enumerate(others(place, half)):
            started.append(
                copy_to(
                    "col", 2 * peer + parity, mine.at[h, peer], far.at[h, place], fsend.at[h, k],
                    frecv.at[h, place],
                )
            )
            started[-1].start()
    out_c[...] = dot3(inv, panel_c[...], NN)
    for _ in range(4):
        next(factor, None)

    gathers = [
        Gather(summed.at[h], full.at[h], sems[4 * h : 4 * h + 4], count) for h in range(halves)
    ]
    for h in range(halves):
        total = mine[h, place]
        for peer in others(place, half):
            copy_to(
                "col", 2 * peer + parity, mine.at[h, 0], far.at[h, peer], fsend.at[h, 0],
                frecv.at[h, peer],
            ).wait_recv()
            total = total + far[h, peer]
        summed[h] = total
        gathers[h].start()

    sems = sems[4 * halves :]
    curve[...] = dot3(summed[...].reshape(span, width), vectors, NT)
    curve_sum = RowSum(curve, slots, *sems[:2], row_count)
    curve_gather = Gather(curve_total, curvature, sems[2:6], count)
    curve_sum.start()

    def pass_up(q):
        peer = jnp.minimum(row + 1, row_count - 1)
        return copy_to("row", peer, picked.at[q], picked.at[q], up_send.at[q], precv.at[q])

    def pass_down(q):
        peer = jnp.maximum(row - 1, 0)
        return copy_to("row", peer, picked.at[q], picked.at[q], down_send.at[q], precv.at[q])

    def pass_on(q, go, act):
        pl.when(go & (row >= root) & (row < row_count - 1))(lambda: act(pass_up(q)))
        pl.when(go & (row <= root) & (row > 0))(lambda: act(pass_down(q)))

    def pick(q):
        h, first = chunk_of(q)

        @pl.when(row == root)
        def _():
            for k in range(tile_cols):
                where = pl.ds(pl.multiple_of((k * groups + slot) * tile, tile), tile)
                value = full[h, first : first + per, :, where]
                picked[q, :, k * tile : (k + 1) * tile] = value.reshape(tile // PARTS, tile)

        pass_on(q, row == root, lambda copy: copy.start())

    for h in range(halves):
        gathers[h].finish()
        for q in range(h * PARTS // halves, (h + 1) * PARTS // halves):
            pick(q)
        if h == 0:
            curve_sum.finish()
            curve_total[...] = curve_sum.total()
            curve_gather.start()
    away = jnp.where(row > root, row - root, root - row)
    at_end = (row == 0) | (row == row_count - 1)

    def arrive(q):
        pl.when(row > root)(lambda: pass_down(q).wait_recv())
        pl.when(row < root)(lambda: pass_up(q).wait_recv())

    def relays(due):
        for d in range(1, row_count - 1):
            for q in range(PARTS):
                if due(2 * q + 2 * (d - 1)):

                    @pl.when((away == d) & jnp.logical_not(at_end))
                    def _():
                        arrive(q)
                        pass_on(q, row != root, lambda copy: copy.start())

    hooks = -1
    for hooks, _ in enumerate(factor):
        relays(lambda at: at == hooks)
        if hooks == 1:
            curve_gather.finish()
    relays(lambda at: at > hooks)
    inv2 = work[:, tile:]
    reflect = dot(inv2, dot(inv2, block, NT), TN)
    reflector[...] = reflect
    pieces = curvature[...]
    curvature_t = jnp.concatenate(
        [pieces[:, h * sub : (h + 1) * sub].reshape(tile // halves, tile) for h in range(halves)],
        axis=0,
    )
    both = dot(reflect, inv, TN)
    mixed = -0.5 * dot(dot(both, curvature_t, NN), reflect, NN)
    update_r[...] = dot3(both, full[...].reshape(tile, width), NN) + dot3(mixed, vectors, NN)
    for q in range(PARTS):
        pl.when(at_end)(lambda: arrive(q))
    update_c[...] = dot3(both, picked[...].reshape(tile, -1), NN) + dot3(mixed, out_c[...], NN)
    out_mine[...] = out_r[pl.ds(pl.multiple_of(col * span, span), span), :]

    for q in range(PARTS):
        pass_on(q, row >= 0, lambda copy: copy.wait_send())
    curve_sum.drain()
    for each in (*gathers, curve_gather):
        each.drain()
    for copy in started:
        copy.wait_send()


def read_matrix(lines, rows, tile, row_count, count, tile_cols):
    row, col = lax.axis_index("row"), lax.axis_index("col")
    strips = tile_cols * tile // 128
    matrix = jnp.concatenate(
        [lines[pl.ds(k, rows, stride=strips), :] for k in range(strips)], axis=1
    )
    r = lax.broadcasted_iota(jnp.int32, matrix.shape, 0)
    c = lax.broadcasted_iota(jnp.int32, matrix.shape, 1)
    global_row = (r // tile * row_count + row) * tile + r % tile
    global_col = (c // tile * count + col) * tile + c % tile
    return matrix, global_row, global_col


def product_step(lines, panel_r, panel_c, top, inverse, mirror, row_count, count, groups, tile_cols):
    tile, width = panel_r.shape
    cols = panel_c.shape[1]
    span, half = tile // count, count // 2
    halves = 4 if span % 32 == 0 else 1
    sub = span // halves
    part = (PARTS, tile // PARTS, cols)
    return pl.pallas_call(
        functools.partial(product_kernel, row_count, count, groups, tile_cols),
        out_shape=[
            shape(tile, width),
            shape(tile, cols),
            shape(tile, width),
            shape(tile, cols),
            shape(tile, tile),
            shape(span, width),
        ],
        in_specs=in_vmem(6),
        out_specs=in_vmem(6),
        scratch_shapes=[
            VMEM((halves, count, sub, width), F32),
            VMEM((halves, half, sub, width), F32),
            VMEM((halves, half, sub, width), F32),
            VMEM((halves, half, sub, width), F32),
            VMEM((halves, sub, width), F32),
            VMEM((halves, count, sub, width), F32),
            VMEM(part, F32),
            VMEM((span, tile), F32),
            VMEM((row_count, span, tile), F32),
            VMEM((span, tile), F32),
            VMEM((count, span, tile), F32),
            VMEM((tile, 2 * tile), F32),
            DMA((halves, half)),
            DMA((halves, half)),
            DMA((halves, half)),
            DMA((halves, half)),
            DMA((PARTS,)),
            DMA((PARTS,)),
            DMA((PARTS,)),
            *(gather_sems(count) * halves),
            *row_sems(row_count),
            *gather_sems(count),
        ],
        compiler_params=params(1),
    )(lines, panel_r, panel_c, top, inverse, mirror)


def update_kernel(
    row_count, count, tile_cols,
    where, lines, yr, xr, yc, xc, band, reflector, mine, out, out_band, out_reflector, out_mine,
):
    tile = yr.shape[0]
    strips = tile_cols * tile // 128
    step = pl.program_id(0)
    left = jnp.concatenate([yr[...], xr[...]], axis=0)
    right = jnp.concatenate([xc[...], yc[...]], axis=0)
    correction = dot3(left, right, TN)
    r = lax.broadcasted_iota(jnp.int32, (tile, 128), 0)
    c = lax.broadcasted_iota(jnp.int32, (tile, 128), 1)
    global_row = (step * row_count + where[0]) * tile + r
    for k in range(strips):
        first = (k * 128 // tile * count + where[1]) * tile + k * 128 % tile
        rows = pl.ds(k, tile, stride=strips)
        value = lines[rows, :] - correction[:, k * 128 : (k + 1) * 128]
        out[rows, :] = jnp.where(global_row >= first + c, value, 0.0)

    @pl.when(step == 0)
    def _():
        out_band[...] = band[...]
        out_reflector[...] = reflector[...]
        span, width = mine.shape
        for k in range(width // 128):
            rows = pl.ds(k, span, stride=width // 128)
            out_mine[rows, :] = mine[:, k * 128 : (k + 1) * 128]


def update_step(where, lines, yr, xr, yc, xc, rest, row_count, count, tile_cols):
    tile, width = yr.shape
    steps = width // tile
    block = (lines.shape[0] // steps, 128)
    strip = pl.BlockSpec((tile, tile), lambda i: (0, i))
    band, reflector, mine = rest
    mine_lines = shape(mine.size // 128, 128)

    def whole(array):
        return pl.BlockSpec(array.shape, lambda i: (0, 0))

    lined = pl.BlockSpec(block, lambda i: (i, 0))
    return pl.pallas_call(
        functools.partial(update_kernel, row_count, count, tile_cols),
        grid=(steps,),
        out_shape=[shape(*lines.shape), shape(tile, tile), shape(tile, tile), mine_lines],
        in_specs=[
            pl.BlockSpec(memory_space=pltpu.SMEM), lined, strip, strip, whole(yc), whole(xc),
            whole(band), whole(reflector), whole(mine),
        ],
        out_specs=[lined, whole(band), whole(reflector), whole(mine_lines)],
        compiler_params=params(),
    )(where, lines, yr, xr, yc, xc, band, reflector, mine)


def body(matrix, panel_t):
    tile_rows, _, tile, tile_cols = matrix.shape[:4]
    row_count, count = lax.axis_size("row"), lax.axis_size("col")
    groups = count // row_count
    span, width = tile // count, tile_rows * tile
    lines = matrix.reshape(-1, 128)
    sizes = (row_count, count, groups, tile_cols)
    panel_r, panel_c, top, band, inverse, mirror = panel_step(
        panel_t.reshape(-1, 128), lines, tile, *sizes
    )
    yr, yc, xr, xc, reflector, vectors = product_step(
        lines,
        panel_r.reshape(tile, width),
        panel_c.reshape(tile, -1),
        top.reshape(tile, tile),
        inverse,
        mirror,
        *sizes,
    )
    where = jnp.stack([lax.axis_index("row"), lax.axis_index("col")])
    updated, band, reflector, vectors = update_step(
        where, lines, yr, xr, yc, xc, (band, reflector, vectors), row_count, count, tile_cols
    )
    return (updated.reshape(matrix.shape), vectors.reshape(panel_t.shape), band, reflector)


def solution(mesh):
    placed = (P(None, "row", None, None, "col", None), P("col", None, "row", None))
    return jax.shard_map(
        body,
        mesh=mesh,
        in_specs=placed,
        out_specs=(P(None, "row", None, None, "col", None), P("col", None, "row", None), P(), P()),
        check_vma=False,
    )
```
